512 devices in a mesh: band: 32 (over x, z), grid: 16 (over y, core).
Axes of the slice: x: 4, y: 8, z: 8, core: 2. Of those that a mesh axis runs over, the one named last changes fastest.
Arguments:
- sphere_index: int32 [12288], P('grid'), may hold values from 0 to 16383, as said below
- occupied: float32 [512, 2, 12288], P('band', None, 'grid'), may hold values from -6 to 6
- energies: float32 [32], P('band'), may hold values from -3 to -0.2
- local_pot: float32 [64, 4096], P('grid'), may hold values from 0.5 to 4
- trial_pot: float32 [4, 64, 4096], P(None, 'grid'), may hold values from -24 to 24
Outputs:
- delta_psi: float32 [32, 4, 2, 12288], P('band', None, None, 'grid')
- density: float32 [4, 64, 4096], P(None, 'grid', 'band')
The draws below stay inside these ranges and needn't reach their ends.
Inputs may be any that keep to these rules, and one draw needn't show every extreme that they name: `sphere_index`: for each grid slab g, the 768 entries from g * (768) on are distinct positions p = (kz * 4 + xl) * 64 + ky of that slab, namely those with the smallest f(kx)^2 + f(ky)^2 + f(kz)^2 where kx = g + 16 * xl, listed by rising value with ties broken at random.
All inputs are finite; a program needn't handle non-finite values.
Results may differ from the reference program's by a relative error of at most 0.0001.
Values sent between devices are 32-bit elements; how exact they have to be, the bound alone decides.
A program may use at most 128 MiB of HBM per device.

```python
import math
import jax
import jax.numpy as jnp
from jax import lax

NG = 64
NPW = 12288
OCC = 512
PERTS = 4
ITERS = 2
SOLVE = 32
N_GRID = 16


def wave_number_drawn(wave_index):
    return jnp.where(wave_index < NG // 2, wave_index, wave_index - NG)


def draw_sphere_index(key, part):
    key = jax.random.fold_in(key, 7)
    row_count = NG // N_GRID
    slab_size = NG * row_count * NG
    slab_npw = NPW // N_GRID
    position = jnp.arange(slab_size, dtype=jnp.int32)
    wave_z = position // (row_count * NG)
    row_local = position // NG % row_count
    wave_y = position % NG
    pieces = []
    for owner_rank in range(N_GRID):
        wave_x = owner_rank + N_GRID * row_local
        radius = wave_number_drawn(wave_x) ** 2 + wave_number_drawn(wave_y) ** 2 + wave_number_drawn(wave_z) ** 2
        shuffle = jax.random.permutation(jax.random.fold_in(key, owner_rank), slab_size).astype(jnp.int32)
        scores = radius * slab_size + shuffle
        ranking = jnp.argsort(scores, stable=True)
        pieces.append(ranking[:slab_npw].astype(jnp.int32))
    return jnp.concatenate(pieces)


def shard_levels(stream_key, extent, cuts, low, high):
    gain, own = 1.0, jax.random.fold_in(stream_key, 6)
    for dim, parts in cuts:
        heights = jnp.exp(jax.random.uniform(jax.random.fold_in(own, dim), (parts,), jnp.float32, low / len(cuts), high / len(cuts)))
        gain = gain * jnp.repeat(heights, extent[dim] // parts).reshape([-1 if axis == dim else 1 for axis in range(len(extent))])
    return gain


def normal_values(own_key, extent, scale, most, cuts=(), held_as=jnp.bfloat16):
    entries = jax.random.normal(own_key, extent, jnp.float32) * scale
    if len(cuts) > 0:
        entries = shard_levels(own_key, extent, cuts, -0.22, 0.18) * entries
    return jnp.clip(entries, min=-most, max=most).astype(held_as)


def setup_inputs(seed: int = 0) -> dict:
    streams_of = jax.random.split(jax.random.key(seed), 6)
    sphere_index = draw_sphere_index(jax.random.fold_in(streams_of[5], 71), 0)
    occupied = normal_values(streams_of[1], (OCC, 2, NPW), 1.0, 6.0, ((0, 32), (2, 16)), jnp.float32)
    energies = jnp.clip(-3.0 + 2.8 * jax.random.uniform(streams_of[2], (SOLVE,), jnp.float32) ** shard_levels(streams_of[2], (SOLVE,), ((0, 32),), -0.2, 0.2), -3.0, -0.2)
    local_pot = jnp.clip(jnp.exp(math.log(4.0) - 2.0794415 * jax.random.uniform(streams_of[3], (NG, NG * NG), jnp.float32) ** shard_levels(streams_of[3], (NG, NG * NG), ((0, 16),), -0.2, 0.2)), 0.5, 4.0)
    trial_pot = normal_values(streams_of[4], (PERTS, NG, NG * NG), 4.0, 24.0, ((1, 16),), jnp.float32)
    return {"sphere_index": sphere_index, "occupied": occupied, "energies": energies, "local_pot": local_pot, "trial_pot": trial_pot}


KIN_SCALE = 0.02
SHIFT_WEIGHT = 2.0
PRECISE = lax.Precision.HIGHEST

def wave_number(wave_index):
    return jnp.where(wave_index < NG // 2, wave_index, wave_index - NG)

def reference(sphere_index, occupied, energies, local_pot, trial_pot):
    slab_npw = NPW // N_GRID
    row_count = NG // N_GRID
    volume = NG * NG * NG
    owner_slab = jnp.arange(NPW, dtype=jnp.int32) // slab_npw
    wave_z = sphere_index // (row_count * NG)
    row_local = sphere_index // NG % row_count
    wave_y = sphere_index % NG
    wave_x = owner_slab + N_GRID * row_local
    full_pos = ((wave_z * NG + wave_x) * NG + wave_y).astype(jnp.int32)
    kinetic = KIN_SCALE * (wave_number(wave_x) ** 2 + wave_number(wave_y) ** 2 + wave_number(wave_z) ** 2).astype(jnp.float32)
    basis_norm = 2.0 * NPW
    potential = local_pot.reshape(NG, NG, NG)
    trials = trial_pot.reshape(PERTS, NG, NG, NG)

    def to_grid(coeffs):
        batch = coeffs.shape[0]
        real_part = jnp.zeros((batch, volume), jnp.float32).at[:, full_pos].set(coeffs[:, 0])
        imag_part = jnp.zeros((batch, volume), jnp.float32).at[:, full_pos].set(coeffs[:, 1])
        spectrum = lax.complex(real_part, imag_part).reshape(batch, NG, NG, NG)
        return jnp.fft.ifftn(spectrum, axes=(1, 2, 3)) * math.sqrt(volume)

    def to_sphere(real_field):
        batch = real_field.shape[0]
        spectrum = jnp.fft.fftn(real_field, axes=(1, 2, 3)).reshape(batch, volume)[:, full_pos] / math.sqrt(volume)
        return jnp.stack([jnp.real(spectrum), jnp.imag(spectrum)], axis=1)

    def swap_pair(vector):
        return jnp.stack([vector[:, 1], -vector[:, 0]], axis=1)

    def project(vector):
        correlation_re = jnp.einsum('bkj,okj->bo', vector, occupied, precision=PRECISE)
        correlation_im = jnp.einsum('bkj,okj->bo', swap_pair(vector), occupied, precision=PRECISE)
        direct = jnp.einsum('bo,okj->bkj', correlation_re, occupied, precision=PRECISE)
        turned = jnp.einsum('bo,okj->bkj', correlation_im, occupied, precision=PRECISE)
        return (direct + jnp.stack([-turned[:, 1], turned[:, 0]], axis=1)) / basis_norm

    def one_band(density, band_index):
        own_band = lax.dynamic_slice_in_dim(occupied, band_index, 1, 0)
        energy = lax.dynamic_slice_in_dim(energies, band_index, 1, 0)
        own_real = to_grid(own_band)
        source = to_sphere(trials * own_real)
        right_side = project(source) - source

        def operate(vector):
            potential_term = to_sphere(potential[None] * to_grid(vector))
            return kinetic * vector + potential_term - energy[0] * vector + SHIFT_WEIGHT * project(vector)
        solution = jnp.zeros_like(right_side)
        residual = right_side
        direction = right_side
        norm_now = lax.optimization_barrier(jnp.sum(residual * residual, axis=(1, 2)))
        for iteration in range(ITERS):
            image = operate(direction)
            step_size = norm_now / lax.optimization_barrier(jnp.sum(direction * image, axis=(1, 2)))
            solution = solution + step_size[:, None, None] * direction
            residual = residual - step_size[:, None, None] * image
            if iteration + 1 < ITERS:
                norm_next = lax.optimization_barrier(jnp.sum(residual * residual, axis=(1, 2)))
                direction = residual + (norm_next / norm_now)[:, None, None] * direction
                norm_now = norm_next
        response = to_grid(solution)
        density_term = 2.0 * jnp.real(jnp.conj(own_real) * response)
        return (density + density_term.reshape(PERTS, NG, NG * NG), solution)
    start = jnp.zeros((PERTS, NG, NG * NG), jnp.float32)
    density, responses = lax.scan(one_band, start, jnp.arange(SOLVE, dtype=jnp.int32))
    return (responses, density)
```

```python
import numpy as np
import jax
import jax.numpy as jnp
import ml_dtypes
from jax import lax
from jax.experimental import pallas as pl
from jax.experimental.pallas import tpu as pltpu
from jax.sharding import PartitionSpec as P

NG = 64
NPW = 12288
NJ = 768
PERTS = 4
GRID = 16
XS, ZS = 4, 8
BANDS = 32
KIN_SCALE = 0.02
MESH = pl.DeviceIdType.MESH
F32 = jnp.float32
BF16 = jnp.bfloat16


def halves(table):
    high = table.astype(ml_dtypes.bfloat16)
    low = (table - high.astype(np.float64)).astype(ml_dtypes.bfloat16)
    return high, low


def make_tables():
    freq = np.arange(32) - 32 * (np.arange(32) >= 16)
    norm = 1.0 / np.sqrt(NG)
    angle = 2 * np.pi / NG
    phase = np.exp(1j * angle * np.outer(np.arange(NG), freq)) * norm
    z_tab = np.zeros((NG, 2, 2, 32))
    for ri in range(2):
        value = phase * (1j**ri)
        z_tab[:, 0, ri], z_tab[:, 1, ri] = value.real, value.imag
    z_tab = z_tab.reshape(128, 64)
    y_tab = np.zeros((PERTS, 2, 32, 2, 2, PERTS, NG))
    own_tab = np.zeros((2, 2, 32, 2, 2, PERTS, NG))
    for p in range(PERTS):
        for k in range(2):
            y_tab[p, k, :, k, 0, p] = phase.real.T
            y_tab[p, k, :, k, 1, p] = phase.imag.T
            own_tab[0, k, :, k, 0, p] = phase.real.T
            own_tab[0, k, :, k, 1, p] = phase.imag.T
    y_tab = y_tab.reshape(256, 1024)
    own_tab = own_tab.reshape(128, 1024)
    x_tab = np.zeros((2, 32, 2, 4, 2, 2, GRID, 4, 2))
    for k in range(2):
        rotor = np.exp(1j * angle * np.outer(np.arange(NG), np.arange(GRID) - 16 * k)) * norm
        rotor = rotor.reshape(32, 2, GRID)
        for cs in range(2):
            for ri in range(2):
                value = rotor * (1j ** (cs + ri))
                for zl in range(4):
                    x_tab[0, :, :, zl, k, cs, :, zl, ri] = value.real
                    x_tab[1, :, :, zl, k, cs, :, zl, ri] = value.imag
    x_tab = x_tab.reshape(512, 512)
    tables = []
    for table in (z_tab, y_tab, own_tab, x_tab, x_tab.T):
        tables.extend(halves(table))
    return tables


def split(value):
    high = value.astype(BF16)
    return high, (value - high.astype(F32)).astype(BF16)


def dot(a, b, ca, cb):
    return lax.dot_general(a, b, (((ca,), (cb,)), ((), ())), preferred_element_type=F32)


def dot3(a_high, a_low, b_high, b_low, ca=1, cb=0):
    total = dot(a_high, b_high, ca, cb) + dot(a_low, b_high, ca, cb)
    return total + dot(a_high, b_low, ca, cb)


def turn(vector):
    return jnp.concatenate([-vector[:, NJ:], vector[:, :NJ]], axis=1)


def kernel(
    sph, occ, energy, pot, trial,
    zt_hi, zt_lo, y_hi, y_lo, o_hi, o_lo, t_hi, t_lo, tt_hi, tt_lo,
    dpsi, dens,
    gath, gath_hi, gath_lo, own, ztab_hi, ztab_lo, col_mask, rhs_hi, rhs_lo,
    own_send, own_recv, send, recv, tile_send, tile_recv, full_send, full_recv, sum_send, sum_recv,
    den_send, den_recv, own_field, field, ssem, rsem, gsend, grecv,
):
    g = lax.axis_index("grid")
    r = lax.axis_index("band")
    bx, bz = r // ZS, r % ZS

    barrier = pltpu.get_barrier_semaphore()

    def greet_grid(k, carry):
        pl.semaphore_signal(barrier, inc=1, device_id={"grid": (g + k) % GRID}, device_id_type=MESH)
        return carry

    def greet_band(k, carry):
        pl.semaphore_signal(barrier, inc=1, device_id={"band": (r + k) % BANDS}, device_id_type=MESH)
        return carry

    lax.fori_loop(1, GRID, greet_grid, 0)
    lax.fori_loop(1, BANDS, greet_band, 0)

    def taken(ref, sem):
        pltpu.make_async_copy(ref, ref, sem).wait()

    def to_band(src, dst, send_sem, recv_sem, x, z):
        pltpu.make_async_remote_copy(
            src_ref=src, dst_ref=dst, send_sem=send_sem, recv_sem=recv_sem,
            device_id={"band": x * ZS + z}, device_id_type=MESH,
        ).start()

    place = sph[...]
    kz, xl, ky = place // 256, (place // 64) % 4, place % 64
    kx = g + 16 * xl

    def wave(k):
        return jnp.where(k < 32, k, k - 64)

    fx, fy, fz = wave(kx), wave(ky), wave(kz)
    kinetic = KIN_SCALE * (fx * fx + fy * fy + fz * fz).astype(F32)
    diag = jnp.concatenate([kinetic, kinetic], axis=1) - energy[0, 0]
    one_z = jnp.where(lax.broadcasted_iota(jnp.int32, (32, NJ), 0) == (kz & 31), 1.0, 0.0).astype(BF16)
    column = (xl >> 1) * 32 + (ky & 31)
    one_col = jnp.where(lax.broadcasted_iota(jnp.int32, (64, NJ), 0) == column, 1.0, 0.0)
    col_mask[:, :NJ] = one_col
    col_mask[:, NJ:] = one_col
    for ri in range(2):
        lanes = pl.ds(ri * NJ, NJ)
        ztab_hi[:, lanes] = dot(zt_hi[:, 32 * ri : 32 * ri + 32], one_z, 1, 0).astype(BF16)
        ztab_lo[:, lanes] = dot(zt_lo[:, 32 * ri : 32 * ri + 32], one_z, 1, 0).astype(BF16)
    own_z = pl.ds(pl.multiple_of(8 * bz, 8), 8)
    for part in range(2):
        for ri in range(2):
            gath[part, bx, own_z, NJ * ri : NJ * ri + NJ] = occ[8 * part : 8 * part + 8, ri, :]

    pl.semaphore_wait(barrier, GRID - 1 + BANDS - 1)

    @pl.when(r == 0)
    def _():
        pltpu.make_async_copy(occ.at[0], own, rsem.at[0]).start()

    @pl.when(r < 2)
    def _():
        def give(i, carry):
            pltpu.make_async_remote_copy(
                src_ref=occ.at[i], dst_ref=own, send_sem=ssem.at[0], recv_sem=rsem.at[0],
                device_id={"band": 16 * r + i}, device_id_type=MESH,
            ).start()
            return carry

        lax.fori_loop(jnp.where(r == 0, 1, 0), 16, give, 0)

    def block(part, x, z):
        return gath.at[part, x, pl.ds(pl.multiple_of(8 * z, 8), 8)]

    def col(z, first=0, count=XS):
        return gath.at[0, pl.ds(first, count), pl.ds(pl.multiple_of(8 * z, 8), 8)]

    z_up, z_dn = (bz + 1) % ZS, (bz + ZS - 1) % ZS

    def across(part, z, slot):
        for k in range(1, XS):
            to_band(block(part, bx, z), block(part, bx, z), gsend.at[slot], grecv.at[slot], (bx + k) % XS, bz)

    def gather_0():
        across(0, bz, 0)
        to_band(block(1, bx, bz), block(1, bx, bz), gsend.at[3], grecv.at[10], bx, z_up)
        to_band(block(1, bx, bz), block(1, bx, bz), gsend.at[3], grecv.at[11], bx, z_dn)
        across(1, bz, 1)

    def gather_1():
        taken(gath.at[0, pl.ds(0, 3), pl.ds(0, 8)], grecv.at[0])
        to_band(col(bz), col(bz), gsend.at[2], grecv.at[2], bx, z_up)
        to_band(col(bz), col(bz), gsend.at[2], grecv.at[3], bx, z_dn)
        gather_part1(1)

    def gather_part1(d):
        below, above = (bz + ZS - d) % ZS, (bz + d) % ZS
        taken(block(1, bx, below), grecv.at[8 + 2 * d])
        to_band(block(1, bx, below), block(1, bx, below), gsend.at[3], grecv.at[10 + 2 * d], bx, z_up)
        taken(block(1, bx, above), grecv.at[9 + 2 * d])
        if d < 3:
            to_band(block(1, bx, above), block(1, bx, above), gsend.at[3], grecv.at[11 + 2 * d], bx, z_dn)
        across(1, below, 1)
        across(1, above, 1)

    def gather_mid(d):
        below, above = (bz + ZS - d + 1) % ZS, (bz + d - 1) % ZS
        taken(col(below), grecv.at[2 * d - 2])
        to_band(col(below), col(below), gsend.at[2], grecv.at[2 * d], bx, z_up)
        taken(col(above), grecv.at[2 * d - 1])
        to_band(col(above), col(above), gsend.at[2], grecv.at[2 * d + 1], bx, z_dn)
        gather_part1(d)

    def gather_4():
        below, above = (bz + ZS - 3) % ZS, (bz + 3) % ZS
        taken(col(below), grecv.at[6])
        to_band(col(below, 0, 2), col(below, 0, 2), gsend.at[2], grecv.at[8], bx, z_up)
        taken(col(above), grecv.at[7])
        to_band(col(above, 2, 2), col(above, 2, 2), gsend.at[2], grecv.at[9], bx, z_dn)
        far = (bz + 4) % ZS
        taken(block(1, bx, far), grecv.at[16])
        across(1, far, 1)

    def gather_5():
        far = (bz + 4) % ZS
        taken(col(far, 0, 2), grecv.at[8])
        taken(col(far, 2, 2), grecv.at[9])
        taken(gath.at[1, pl.ds(0, 3)], grecv.at[1])

    def exchange(src, dst, slot):
        def go(k, carry):
            peer = (g + k) % GRID
            pltpu.make_async_remote_copy(
                src_ref=src.at[pl.ds(pl.multiple_of(8 * peer, 8), 8)],
                dst_ref=dst.at[pl.ds(pl.multiple_of(8 * g, 8), 8)],
                send_sem=ssem.at[slot], recv_sem=rsem.at[slot],
                device_id={"grid": peer}, device_id_type=MESH,
            ).start()
            return carry

        lax.fori_loop(1, GRID, go, 0)
        here = pl.ds(pl.multiple_of(8 * g, 8), 8)
        dst[here, :] = src[here, :]

    def exchanged(dst, slot):
        taken(dst.at[pl.ds(0, 8 * (GRID - 1))], rsem.at[slot])

    def tiles(n, slot):
        def go(k, carry):
            peer = (g + k) % GRID
            pltpu.make_async_remote_copy(
                src_ref=tile_send.at[n, peer // 4], dst_ref=tile_recv.at[n, g],
                send_sem=ssem.at[slot], recv_sem=rsem.at[slot],
                device_id={"grid": peer}, device_id_type=MESH,
            ).start()
            return carry

        lax.fori_loop(1, GRID, go, 0)
        tile_recv[n, g] = tile_send[n, g // 4]

    def tiles_sum(n, slot):
        taken(tile_recv.at[n, pl.ds(0, GRID - 1)], rsem.at[slot])
        return jnp.sum(tile_recv[n], axis=0)

    def share(n, total, slot):
        quarter = g // 4
        full_send[n] = total
        for k in range(1, 4):
            pltpu.make_async_remote_copy(
                src_ref=full_send.at[n], dst_ref=full_recv.at[n, quarter],
                send_sem=ssem.at[slot], recv_sem=rsem.at[slot],
                device_id={"grid": (g + 4 * k) % GRID}, device_id_type=MESH,
            ).start()
        full_recv[n, quarter] = total

    def shared(n, slot):
        taken(full_recv.at[n, pl.ds(0, 3)], rsem.at[slot])
        return jnp.concatenate([full_recv[n, k] for k in range(4)], axis=1)

    def sums(n, value, slot):
        sum_send[n] = value

        def go(k, carry):
            pltpu.make_async_remote_copy(
                src_ref=sum_send.at[n], dst_ref=sum_recv.at[n, g],
                send_sem=ssem.at[slot], recv_sem=rsem.at[slot],
                device_id={"grid": (g + k) % GRID}, device_id_type=MESH,
            ).start()
            return carry

        lax.fori_loop(1, GRID, go, 0)
        sum_recv[n, g] = value

    def summed(n, slot):
        taken(sum_recv.at[n, pl.ds(0, GRID - 1)], rsem.at[slot])
        return jnp.sum(sum_recv[n], axis=0)

    def spread(rows, count):
        for p in range(count):
            row = rows[p : p + 1]
            high = row.astype(BF16).astype(F32)
            mask = col_mask[...]
            rhs_hi[64 * p : 64 * p + 64, :] = (mask * high).astype(BF16)
            rhs_lo[64 * p : 64 * p + 64, :] = (mask * (row - high)).astype(BF16)
        wide = pl.ds(0, 64 * count)
        return dot3(ztab_hi[...], ztab_lo[...], rhs_hi[wide, :], rhs_lo[wide, :], 1, 1)

    def to_planes(spectral, yh, yl):
        high, low = split(spectral)
        part = dot3(high, low, yh[...], yl[...])
        part = jnp.concatenate([part[:, 256 * k : 256 * k + 256] for k in range(4)], axis=0)
        high, low = split(part)
        return dot3(t_hi[...], t_lo[...], high, low)

    def from_planes(values):
        high, low = split(values)
        part = dot3(tt_hi[...], tt_lo[...], high, low)
        part = jnp.concatenate([part[128 * k : 128 * k + 128] for k in range(4)], axis=1)
        high, low = split(part)
        return dot3(high, low, y_hi[...], y_lo[...], 1, 1)

    sub8 = lax.broadcasted_iota(jnp.int32, (8, 1), 0)

    def pick(spectral):
        high, low = split(jnp.transpose(spectral))
        result = jnp.zeros((8, 2 * NJ), F32)
        for p in range(PERTS):
            rows = slice(64 * p, 64 * p + 64)
            box = dot3(high[rows], low[rows], ztab_hi[...], ztab_lo[...])
            line = jnp.sum(box * col_mask[...], axis=0, keepdims=True)
            result = jnp.where(sub8 == p, line, result)
            result = jnp.where(sub8 == p + 4, -turn(line), result)
        return result

    def correlate(vector, n):
        high = vector.astype(BF16).astype(F32)
        both = jnp.concatenate([high, vector - high], axis=0).astype(BF16)
        first = dot(both, gath_hi[...], 1, 1)
        second = dot(both, gath_lo[...], 1, 1)
        total = first[:8] + first[8:] + second[:8]
        for k in range(4):
            tile_send[n, k] = total[:, 128 * k : 128 * k + 128]

    sign = jnp.where(sub8 < 4, 1.0, -1.0)

    def expand(correlations):
        high = correlations.astype(BF16).astype(F32)
        both = jnp.concatenate([high, correlations - high], axis=0).astype(BF16)
        first = dot(both, gath_hi[...], 1, 0)
        second = dot(both, gath_lo[...], 1, 0)
        direct = first[:8] + first[8:] + second[:8]
        return (direct + sign * turn(pltpu.roll(direct, 4, 0))) * (1.0 / (2.0 * NPW))

    def per_lane(column_values):
        which = lax.broadcasted_iota(jnp.int32, (1, 256), 1) // 64
        result = jnp.zeros((1, 256), F32)
        for p in range(PERTS):
            result = jnp.where(which == p, column_values[p : p + 1, 0:1], result)
        return result

    def over_lanes(value):
        return jnp.sum(value, axis=1, keepdims=True)

    gather_0()
    taken(own, rsem.at[0])
    own_row = jnp.concatenate([own[0:1, :], own[1:2, :]], axis=1)
    own_send[...] = spread(jnp.concatenate([own_row, own_row], axis=0), 2)
    exchange(own_send, own_recv, 1)
    gather_1()
    exchanged(own_recv, 1)
    own_field[...] = to_planes(own_recv[...], o_hi, o_lo)

    weight = trial[...]
    send[0] = from_planes(jnp.concatenate([own_field[:256] * weight, own_field[256:] * weight], axis=0))
    exchange(send.at[0], recv.at[0], 2)
    gather_mid(2)
    gather_mid(3)
    exchanged(recv.at[0], 2)
    source = pick(recv[0])
    gather_4()
    gather_5()

    def round_pair(k, carry):
        rows = pl.ds(pl.multiple_of(16 * k, 16), 16)
        high, low = split(gath[k // 16, (k // 4) % 4, pl.ds(pl.multiple_of(16 * (k % 4), 16), 16), :])
        gath_hi[rows, :] = high
        gath_lo[rows, :] = low
        return carry

    lax.fori_loop(0, 32, round_pair, 0)
    correlate(source, 0)
    tiles(0, 3)
    share(0, tiles_sum(0, 3), 4)
    direction = expand(shared(0, 4)) - source

    send[1] = spread(direction, PERTS)
    exchange(send.at[1], recv.at[1], 5)
    correlate(direction, 1)
    tiles(1, 6)
    exchanged(recv.at[1], 5)
    field[0] = to_planes(recv[1], y_hi, y_lo)
    local = pot[...]
    send[2] = from_planes(jnp.concatenate([field[0, :256] * local, field[0, 256:] * local], axis=0))
    exchange(send.at[2], recv.at[2], 7)
    corr_dir = tiles_sum(1, 6)
    share(1, corr_dir, 8)
    image = diag * direction + 2.0 * expand(shared(1, 8))
    exchanged(recv.at[2], 7)
    image = image + pick(recv[2])

    send[3] = spread(image, PERTS)
    exchange(send.at[3], recv.at[3], 9)
    lane = lax.broadcasted_iota(jnp.int32, (8, 128), 1)
    dots = jnp.where(lane == 0, over_lanes(direction * direction), 0.0)
    dots = jnp.where(lane == 1, over_lanes(direction * image), dots)
    dots = jnp.where(lane == 2, over_lanes(image * image), dots)
    sums(0, dots, 10)
    correlate(image, 2)
    tiles(2, 11)
    exchanged(recv.at[3], 9)
    field[1] = to_planes(recv[3], y_hi, y_lo)
    dots = summed(0, 10)
    norm = dots[:, 0:1]
    step0 = norm / dots[:, 1:2]
    norm_next = step0 * step0 * dots[:, 2:3] - norm
    grow = 1.0 + norm_next / norm
    direction1 = grow * direction - step0 * image
    field[1] = per_lane(grow) * field[0] - per_lane(step0) * field[1]
    corr_dir1 = grow * corr_dir - step0 * tiles_sum(2, 11)

    energy_terms = over_lanes(diag * direction1 * direction1)
    corr_terms = over_lanes(corr_dir1 * corr_dir1)
    corr_terms = corr_terms + pltpu.roll(jnp.broadcast_to(corr_terms, (8, 128)), 4, 0)[:, 0:1]
    energy_terms = energy_terms + corr_terms * (2.0 / (2.0 * NPW) / 4.0)
    real, imag = field[1, :256], field[1, 256:]
    squares = jnp.sum(local * (real * real + imag * imag), axis=0, keepdims=True)
    for p in range(PERTS):
        piece = over_lanes(squares[:, 64 * p : 64 * p + 64])
        energy_terms = energy_terms + jnp.where((sub8 % 4) == p, piece, 0.0)
    sums(1, jnp.broadcast_to(energy_terms, (8, 128)), 12)
    own_re, own_im = own_field[:256], own_field[256:]
    dens0 = own_re * field[0, :256] + own_im * field[0, 256:]
    dens1 = own_re * real + own_im * imag
    dens0 = 2.0 * per_lane(step0) * dens0
    step1 = norm_next / summed(1, 12)[:, 0:1]
    den_send[...] = dens0 + 2.0 * per_lane(step1) * dens1

    def give_density(k, carry):
        peer = (r + k) % BANDS
        pltpu.make_async_remote_copy(
            src_ref=den_send.at[pl.ds(pl.multiple_of(8 * peer, 8), 8)],
            dst_ref=den_recv.at[pl.ds(pl.multiple_of(8 * r, 8), 8)],
            send_sem=ssem.at[13], recv_sem=rsem.at[13],
            device_id={"band": peer}, device_id_type=MESH,
        ).start()
        return carry

    lax.fori_loop(1, BANDS, give_density, 0)
    here = pl.ds(pl.multiple_of(8 * r, 8), 8)
    den_recv[here, :] = den_send[here, :]
    response = step0 * direction + step1 * direction1
    for ri in range(2):
        dpsi[0, :, ri, :] = response[:PERTS, NJ * ri : NJ * ri + NJ]

    @pl.when(r == 0)
    def _():
        taken(occ.at[pl.ds(0, 15)], ssem.at[0])

    @pl.when(r == 1)
    def _():
        taken(occ, ssem.at[0])

    taken(own_send.at[pl.ds(0, 120)], ssem.at[1])
    for n, slot in ((0, 2), (1, 5), (2, 7), (3, 9)):
        taken(send.at[n, pl.ds(0, 120)], ssem.at[slot])
    for n, slot in ((0, 3), (1, 6), (2, 11)):
        taken(tile_recv.at[n, pl.ds(0, 15)], ssem.at[slot])
    for n, slot in ((0, 4), (1, 8)):
        taken(full_recv.at[n, pl.ds(0, 3)], ssem.at[slot])
    for n, slot in ((0, 10), (1, 12)):
        taken(sum_recv.at[n, pl.ds(0, 15)], ssem.at[slot])
    taken(gath.at[0, pl.ds(0, 3), pl.ds(0, 8)], gsend.at[0])
    taken(gath.at[1, pl.ds(0, 3)], gsend.at[1])
    taken(gath.at[0, :, pl.ds(0, 56)], gsend.at[2])
    taken(gath.at[0, 0, pl.ds(0, 56)], gsend.at[3])

    taken(den_recv.at[pl.ds(0, 8 * (BANDS - 1))], rsem.at[13])
    total = jnp.zeros((8, 256), F32)
    for k in range(BANDS):
        total = total + den_recv[8 * k : 8 * k + 8, :]
    for p in range(PERTS):
        for half in range(2):
            dens[p, :, 64 * half : 64 * half + 64] = total[4 * half : 4 * half + 4, 64 * p : 64 * p + 64]
    taken(den_send.at[pl.ds(0, 8 * (BANDS - 1))], ssem.at[13])


def on_device(sphere_index, occupied, energies, local_pot, trial_pot):
    trial = trial_pot.reshape(PERTS, 4, 32, 2, NG).transpose(2, 3, 1, 0, 4).reshape(256, 256)
    pot = local_pot.reshape(4, 32, 2, 1, NG).transpose(1, 2, 0, 3, 4)
    pot = jnp.broadcast_to(pot, (32, 2, 4, PERTS, NG)).reshape(256, 256)
    tables = [jnp.asarray(table) for table in make_tables()]
    vmem = pl.BlockSpec(memory_space=pltpu.VMEM)
    smem = pl.BlockSpec(memory_space=pltpu.SMEM)
    scratch = [
        pltpu.VMEM((2, XS, 64, 2 * NJ), F32),
        pltpu.VMEM((512, 2 * NJ), BF16),
        pltpu.VMEM((512, 2 * NJ), BF16),
        pltpu.VMEM((2, NJ), F32),
        pltpu.VMEM((128, 2 * NJ), BF16),
        pltpu.VMEM((128, 2 * NJ), BF16),
        pltpu.VMEM((64, 2 * NJ), F32),
        pltpu.VMEM((256, 2 * NJ), BF16),
        pltpu.VMEM((256, 2 * NJ), BF16),
        pltpu.VMEM((128, 128), F32),
        pltpu.VMEM((128, 128), F32),
        pltpu.VMEM((4, 128, 256), F32),
        pltpu.VMEM((4, 128, 256), F32),
        pltpu.VMEM((3, 4, 8, 128), F32),
        pltpu.VMEM((3, GRID, 8, 128), F32),
        pltpu.VMEM((2, 8, 128), F32),
        pltpu.VMEM((2, 4, 8, 128), F32),
        pltpu.VMEM((2, 8, 128), F32),
        pltpu.VMEM((2, GRID, 8, 128), F32),
        pltpu.VMEM((256, 256), F32),
        pltpu.VMEM((256, 256), F32),
        pltpu.VMEM((512, 256), F32),
        pltpu.VMEM((2, 512, 256), F32),
        pltpu.SemaphoreType.DMA((14,)),
        pltpu.SemaphoreType.DMA((14,)),
        pltpu.SemaphoreType.DMA((4,)),
        pltpu.SemaphoreType.DMA((17,)),
    ]
    return pl.pallas_call(
        kernel,
        out_shape=(
            jax.ShapeDtypeStruct((1, PERTS, 2, NJ), F32),
            jax.ShapeDtypeStruct((PERTS, 4, 128), F32),
        ),
        in_specs=[vmem, vmem, smem] + [vmem] * 12,
        out_specs=(vmem, vmem),
        scratch_shapes=scratch,
        compiler_params=pltpu.CompilerParams(
            collective_id=0, has_side_effects=True, vmem_limit_bytes=56 * 1024 * 1024
        ),
        name="response",
    )(sphere_index.reshape(1, NJ), occupied, energies.reshape(1, 1), pot, trial, *tables)


def solution(mesh):
    return jax.shard_map(
        on_device,
        mesh=mesh,
        in_specs=(
            P("grid"),
            P("band", None, "grid"),
            P("band"),
            P("grid", None),
            P(None, "grid", None),
        ),
        out_specs=(P("band", None, None, "grid"), P(None, "grid", "band")),
        check_vma=False,
    )
```

```python
import numpy as np
import jax
import jax.numpy as jnp
import ml_dtypes
from jax import lax
from jax.experimental import pallas as pl
from jax.experimental.pallas import tpu as pltpu
from jax.sharding import PartitionSpec as P

NG = 64
NPW = 12288
NJ = 768
PERTS = 4
GRID = 16
XS, ZS = 4, 8
BANDS = 32
KIN_SCALE = 0.02
MESH = pl.DeviceIdType.MESH
F32 = jnp.float32
BF16 = jnp.bfloat16


def halves(table):
    high = table.astype(ml_dtypes.bfloat16)
    low = (table - high.astype(np.float64)).astype(ml_dtypes.bfloat16)
    return high, low


def make_tables():
    freq = np.arange(32) - 32 * (np.arange(32) >= 16)
    norm = 1.0 / np.sqrt(NG)
    angle = 2 * np.pi / NG
    phase = np.exp(1j * angle * np.outer(np.arange(NG), freq)) * norm
    z_tab = np.zeros((NG, 2, 2, 32))
    for ri in range(2):
        value = phase * (1j**ri)
        z_tab[:, 0, ri], z_tab[:, 1, ri] = value.real, value.imag
    z_tab = z_tab.reshape(128, 64)
    y_tab = np.zeros((PERTS, 2, 32, 2, 2, PERTS, NG))
    own_tab = np.zeros((2, 2, 32, 2, 2, PERTS, NG))
    for p in range(PERTS):
        for k in range(2):
            y_tab[p, k, :, k, 0, p] = phase.real.T
            y_tab[p, k, :, k, 1, p] = phase.imag.T
            own_tab[0, k, :, k, 0, p] = phase.real.T
            own_tab[0, k, :, k, 1, p] = phase.imag.T
    y_tab = y_tab.reshape(256, 1024)
    own_tab = own_tab.reshape(128, 1024)
    x_tab = np.zeros((2, 32, 2, 4, 2, 2, GRID, 4, 2))
    for k in range(2):
        rotor = np.exp(1j * angle * np.outer(np.arange(NG), np.arange(GRID) - 16 * k)) * norm
        rotor = rotor.reshape(32, 2, GRID)
        for cs in range(2):
            for ri in range(2):
                value = rotor * (1j ** (cs + ri))
                for zl in range(4):
                    x_tab[0, :, :, zl, k, cs, :, zl, ri] = value.real
                    x_tab[1, :, :, zl, k, cs, :, zl, ri] = value.imag
    x_tab = x_tab.reshape(512, 512)
    return list(halves(z_tab)) + [t.astype(np.float32) for t in (own_tab, x_tab, y_tab, x_tab.T, y_tab.T)]


def split(value):
    high = value.astype(BF16)
    return high, (value - high.astype(F32)).astype(BF16)


def dot(a, b, ca, cb):
    return lax.dot_general(a, b, (((ca,), (cb,)), ((), ())), preferred_element_type=F32)


def dot3(a_high, a_low, b_high, b_low, ca=1, cb=0):
    total = dot(a_high, b_high, ca, cb) + dot(a_low, b_high, ca, cb)
    return total + dot(a_high, b_low, ca, cb)


def turn(vector):
    return jnp.concatenate([-vector[:, NJ:], vector[:, :NJ]], axis=1)


def kernel(
    sph, occ, energy, pot_in, trial_in, zt_hi, zt_lo, *refs,
):
    stored, (dpsi, dens), whole, kept, rest = refs[:5], refs[5:7], refs[7:12], refs[12:22], refs[22:]
    o_hi, o_lo, t_hi, t_lo, y_hi, y_lo, tt_hi, tt_lo, yt_hi, yt_lo = kept
    (
    gath, gath_hi, gath_lo, own, ztab_hi, ztab_lo, col_mask, rhs_hi, rhs_lo,
    own_send, own_recv, send, recv, pair_send, pair_recv, half_send, half_recv, full_recv, sum_send, sum_recv,
    den_send, den_recv, own_field, field, pot, trial, ssem, rsem, gsend, grecv, tsem,
    ) = rest
    g = lax.axis_index("grid")
    r = lax.axis_index("band")
    bx, bz = r // ZS, r % ZS
    gy, gc = g // 2, g % 2

    def ring(j, half):
        return half + (1 - 2 * (j % 2)) * ((j + 1) // 2)

    def grid_peer(k):
        return 2 * ((gy + ring(k // 2, 4)) % 8) + (gc + k + 1) % 2

    def band_peer(k):
        return ZS * ((bx + ring(k % 4, 2)) % XS) + (bz + ring(k // 4, 4)) % ZS

    barrier = pltpu.get_barrier_semaphore()

    def greet_grid(k, carry):
        pl.semaphore_signal(barrier, inc=1, device_id={"grid": grid_peer(k)}, device_id_type=MESH)
        return carry

    def greet_band(k, carry):
        pl.semaphore_signal(barrier, inc=1, device_id={"band": band_peer(k)}, device_id_type=MESH)
        return carry

    lax.fori_loop(0, BANDS - 1, greet_band, 0)
    lax.fori_loop(0, GRID - 1, greet_grid, 0)

    loads = [pltpu.make_async_copy(a, b, tsem.at[k]) for k, (a, b) in enumerate(zip(stored, whole))]
    for load in loads:
        load.start()

    def taken(ref, sem):
        pltpu.make_async_copy(ref, ref, sem).wait()

    sent = []

    def drain():
        for ref, sem in sent:
            taken(ref, sem)

    def to_band(src, dst, send_sem, recv_sem, x, z):
        pltpu.make_async_remote_copy(
            src_ref=src, dst_ref=dst, send_sem=send_sem, recv_sem=recv_sem,
            device_id={"band": x * ZS + z}, device_id_type=MESH,
        ).start()

    place = sph[...].reshape(1, NJ)
    kz, xl, ky = place // 256, (place // 64) % 4, place % 64
    kx = g + 16 * xl

    def wave(k):
        return jnp.where(k < 32, k, k - 64)

    fx, fy, fz = wave(kx), wave(ky), wave(kz)
    kinetic = KIN_SCALE * (fx * fx + fy * fy + fz * fz).astype(F32)
    diag = jnp.concatenate([kinetic, kinetic], axis=1) - energy[...].reshape(1, 1)
    one_z = jnp.where(lax.broadcasted_iota(jnp.int32, (32, NJ), 0) == (kz & 31), 1.0, 0.0).astype(BF16)
    column = (xl >> 1) * 32 + (ky & 31)
    one_col = jnp.where(lax.broadcasted_iota(jnp.int32, (64, NJ), 0) == column, 1.0, 0.0)
    col_mask[:, :NJ] = one_col
    col_mask[:, NJ:] = one_col
    for ri in range(2):
        lanes = pl.ds(ri * NJ, NJ)
        ztab_hi[:, lanes] = dot(zt_hi[:, 32 * ri : 32 * ri + 32], one_z, 1, 0).astype(BF16)
        ztab_lo[:, lanes] = dot(zt_lo[:, 32 * ri : 32 * ri + 32], one_z, 1, 0).astype(BF16)
    left = lax.broadcasted_iota(jnp.int32, (4, 128), 1) < 64

    def lay(t, carry):
        lanes = pl.ds(pl.multiple_of(128 * t, 128), 128)
        rows = pl.ds(pl.multiple_of(8 * t, 8), 8)
        for q in range(3):
            a, b = (pot_in[:, lanes],) * 2 if q == 2 else (trial_in[2 * q, :, lanes], trial_in[2 * q + 1, :, lanes])
            even = jnp.where(left, a, pltpu.roll(b, 64, 1))
            odd = jnp.where(left, pltpu.roll(a, 64, 1), b)
            both = jnp.concatenate([even, odd], axis=0)
            if q == 2:
                pot[rows, :] = both
            else:
                trial[rows, 128 * q : 128 * q + 128] = both
        return carry

    lax.fori_loop(0, 32, lay, 0)
    own_z = pl.ds(pl.multiple_of(8 * bz, 8), 8)
    for part in range(2):
        for ri in range(2):
            gath[part, bx, own_z, NJ * ri : NJ * ri + NJ] = occ[8 * part : 8 * part + 8, ri, :]

    for k, load in enumerate(loads):
        load.wait()
        for i in range(0, whole[k].shape[0], 64):
            high, low = split(whole[k][i : i + 64, :])
            kept[2 * k][i : i + 64, :] = high
            kept[2 * k + 1][i : i + 64, :] = low

    pl.semaphore_wait(barrier, GRID - 1 + BANDS - 1)

    @pl.when(r == 0)
    def _():
        pltpu.make_async_copy(occ.at[0], own, rsem.at[0]).start()

    @pl.when(r < 2)
    def _():
        def give(i, carry):
            pltpu.make_async_remote_copy(
                src_ref=occ.at[i], dst_ref=own, send_sem=ssem.at[0], recv_sem=rsem.at[0],
                device_id={"band": 16 * r + i}, device_id_type=MESH,
            ).start()
            return carry

        lax.fori_loop(jnp.where(r == 0, 1, 0), 16, give, 0)

    def drain_own():
        @pl.when(r == 0)
        def _():
            taken(occ.at[pl.ds(0, 15)], ssem.at[0])

        @pl.when(r == 1)
        def _():
            taken(occ, ssem.at[0])

    def block(part, x, z):
        return gath.at[part, x, pl.ds(pl.multiple_of(8 * z, 8), 8)]

    def col(z, first=0, count=XS):
        return gath.at[0, pl.ds(first, count), pl.ds(pl.multiple_of(8 * z, 8), 8)]

    z_up, z_dn = (bz + 1) % ZS, (bz + ZS - 1) % ZS

    def across(part, z, slot):
        for k in (2, 1, 3):
            to_band(block(part, bx, z), block(part, bx, z), gsend.at[slot], grecv.at[slot], (bx + k) % XS, bz)

    def below(d):
        return (bz + ZS - d) % ZS

    def above(d):
        return (bz + d) % ZS

    def first(way, d, half):
        return grecv.at[2 + 7 * way + (6 if d == 4 else 2 * d - 2 + half)]

    def second(way, d):
        return grecv.at[16 + 4 * way + d - 1]

    def send_first(way, z, d, half):
        ref = col(z, 2 * half, 2)
        to_band(ref, ref, gsend.at[2], first(way, d, half), bx, z_dn if way else z_up)

    def send_second(way, z, d):
        to_band(block(1, bx, z), block(1, bx, z), gsend.at[3], second(way, d), bx, z_dn if way else z_up)

    def gather_0():
        across(0, bz, 0)
        for way in range(2):
            send_second(way, bz, 1)
        across(1, bz, 1)
        sent.append((gath.at[0, pl.ds(0, 3), pl.ds(0, 8)], gsend.at[0]))
        sent.append((gath.at[1, pl.ds(0, 3)], gsend.at[1]))
        sent.append((gath.at[0, :, pl.ds(0, 56)], gsend.at[2]))
        sent.append((gath.at[0, 0, pl.ds(0, 56)], gsend.at[3]))

    def gather_1():
        taken(gath.at[0, pl.ds(0, 3), pl.ds(0, 8)], grecv.at[0])
        for half in range(2):
            for way in range(2):
                send_first(way, bz, 1, half)

    def gather_first(d, half):
        for way in range(2):
            z = above(d) if way else below(d)
            if d < 3 or half == way:
                taken(col(z, 2 * half, 2), first(way, d, half))
                send_first(way, z, d + 1, half)

    def gather_second(d):
        for way in range(1 if d == 4 else 2):
            z = above(d) if way else below(d)
            taken(block(1, bx, z), second(way, d))
            if d + way < 4:
                send_second(way, z, d + 1)
            across(1, z, 1)

    def gather_last():
        taken(col(below(3), 2, 2), first(0, 3, 1))
        taken(col(above(3), 0, 2), first(1, 3, 0))
        taken(col(below(4), 0, 2), first(0, 4, 0))
        taken(col(below(4), 2, 2), first(1, 4, 1))
        taken(gath.at[1, pl.ds(0, 3)], grecv.at[1])

    def exchange(src, dst, slot):
        def go(k, carry):
            peer = grid_peer(k)
            pltpu.make_async_remote_copy(
                src_ref=src.at[pl.ds(pl.multiple_of(8 * peer, 8), 8)],
                dst_ref=dst.at[pl.ds(pl.multiple_of(8 * g, 8), 8)],
                send_sem=ssem.at[slot], recv_sem=rsem.at[slot],
                device_id={"grid": peer}, device_id_type=MESH,
            ).start()
            return carry

        lax.fori_loop(0, GRID - 1, go, 0)
        sent.append((src.at[pl.ds(0, 8 * (GRID - 1))], ssem.at[slot]))
        here = pl.ds(pl.multiple_of(8 * g, 8), 8)
        dst[here, :] = src[here, :]

    def exchanged(dst, slot):
        taken(dst.at[pl.ds(0, 8 * (GRID - 1))], rsem.at[slot])

    other = 1 - gc

    def to_other(src, dst, slot):
        pltpu.make_async_remote_copy(
            src_ref=src, dst_ref=dst, send_sem=ssem.at[slot], recv_sem=rsem.at[slot],
            device_id={"grid": 2 * gy + other}, device_id_type=MESH,
        ).start()
        sent.append((src, ssem.at[slot]))

    def across_chip(n, slot):
        to_other(pair_send.at[n, pl.ds(2 * other, 2)], pair_recv.at[n], slot)

    def across_ring(n, slot, slot_in):
        taken(pair_recv.at[n], rsem.at[slot_in])
        total = pair_send[n, pl.ds(2 * gc, 2)] + pair_recv[n]
        half_send[n] = total

        def go(k, carry):
            pltpu.make_async_remote_copy(
                src_ref=half_send.at[n], dst_ref=half_recv.at[n, gy],
                send_sem=ssem.at[slot], recv_sem=rsem.at[slot],
                device_id={"grid": 2 * ((gy + ring(k, 4)) % 8) + gc}, device_id_type=MESH,
            ).start()
            return carry

        lax.fori_loop(0, 7, go, 0)
        sent.append((half_recv.at[n, pl.ds(0, 7)], ssem.at[slot]))
        half_recv[n, gy] = total

    def half_sum(n, slot):
        taken(half_recv.at[n, pl.ds(0, 7)], rsem.at[slot])
        return jnp.sum(half_recv[n], axis=0)

    def share(n, total, slot):
        full_recv[n, pl.ds(2 * gc, 2)] = total
        to_other(full_recv.at[n, pl.ds(2 * gc, 2)], full_recv.at[n, pl.ds(2 * gc, 2)], slot)

    def shared(n, slot):
        taken(full_recv.at[n, pl.ds(0, 2)], rsem.at[slot])
        return jnp.concatenate([full_recv[n, k] for k in range(4)], axis=1)

    def sums(n, value, slot):
        sum_send[n] = value

        def go(k, carry):
            pltpu.make_async_remote_copy(
                src_ref=sum_send.at[n], dst_ref=sum_recv.at[n, g],
                send_sem=ssem.at[slot], recv_sem=rsem.at[slot],
                device_id={"grid": grid_peer(k)}, device_id_type=MESH,
            ).start()
            return carry

        lax.fori_loop(0, GRID - 1, go, 0)
        sent.append((sum_recv.at[n, pl.ds(0, GRID - 1)], ssem.at[slot]))
        sum_recv[n, g] = value

    def summed(n, slot):
        taken(sum_recv.at[n, pl.ds(0, GRID - 1)], rsem.at[slot])
        return jnp.sum(sum_recv[n], axis=0)

    def spread(rows, count):
        for p in range(count):
            row = rows[p : p + 1]
            high = row.astype(BF16).astype(F32)
            mask = col_mask[...]
            rhs_hi[64 * p : 64 * p + 64, :] = (mask * high).astype(BF16)
            rhs_lo[64 * p : 64 * p + 64, :] = (mask * (row - high)).astype(BF16)
        wide = pl.ds(0, 64 * count)
        return dot3(ztab_hi[...], ztab_lo[...], rhs_hi[wide, :], rhs_lo[wide, :], 1, 1)

    def to_planes(spectral, yh, yl):
        high, low = split(spectral)
        part = dot3(high, low, yh[...], yl[...])
        part = jnp.concatenate([part[:, 256 * k : 256 * k + 256] for k in range(4)], axis=0)
        high, low = split(part)
        return dot3(t_hi[...], t_lo[...], high, low)

    def from_planes(values):
        high, low = split(values)
        part = dot3(tt_hi[...], tt_lo[...], high, low)
        part = jnp.concatenate([part[128 * k : 128 * k + 128] for k in range(4)], axis=1)
        high, low = split(part)
        return dot3(high, low, yt_hi[...], yt_lo[...])

    sub8 = lax.broadcasted_iota(jnp.int32, (8, 1), 0)

    def pick(spectral):
        high, low = split(jnp.transpose(spectral))
        result = jnp.zeros((8, 2 * NJ), F32)
        for p in range(PERTS):
            rows = slice(64 * p, 64 * p + 64)
            box = dot3(high[rows], low[rows], ztab_hi[...], ztab_lo[...])
            line = jnp.sum(box * col_mask[...], axis=0, keepdims=True)
            result = jnp.where(sub8 == p, line, result)
            result = jnp.where(sub8 == p + 4, -turn(line), result)
        return result

    def correlate(vector, n):
        high = vector.astype(BF16).astype(F32)
        both = jnp.concatenate([high, vector - high], axis=0).astype(BF16)
        first = dot(both, gath_hi[...], 1, 1)
        second = dot(both, gath_lo[...], 1, 1)
        total = first[:8] + first[8:] + second[:8]
        for k in range(4):
            pair_send[n, k] = total[:, 128 * k : 128 * k + 128]

    sign = jnp.where(sub8 < 4, 1.0, -1.0)

    def expand(correlations):
        high = correlations.astype(BF16).astype(F32)
        both = jnp.concatenate([high, correlations - high], axis=0).astype(BF16)
        first = dot(both, gath_hi[...], 1, 0)
        second = dot(both, gath_lo[...], 1, 0)
        direct = first[:8] + first[8:] + second[:8]
        return (direct + sign * turn(pltpu.roll(direct, 4, 0))) * (1.0 / (2.0 * NPW))

    def per_lane(column_values):
        which = lax.broadcasted_iota(jnp.int32, (1, 256), 1) // 64
        result = jnp.zeros((1, 256), F32)
        for p in range(PERTS):
            result = jnp.where(which == p, column_values[p : p + 1, 0:1], result)
        return result

    def over_lanes(value):
        return jnp.sum(value, axis=1, keepdims=True)

    gather_0()
    taken(own, rsem.at[0])
    own_row = jnp.concatenate([own[0:1, :], own[1:2, :]], axis=1)
    own_send[...] = spread(jnp.concatenate([own_row, own_row], axis=0), 2)
    exchange(own_send, own_recv, 1)
    gather_1()
    gather_second(1)
    gather_first(1, 0)
    gather_second(2)
    gather_first(1, 1)
    exchanged(own_recv, 1)
    own_field[...] = to_planes(own_recv[...], o_hi, o_lo)

    weight = trial[...]
    send[0] = from_planes(jnp.concatenate([own_field[:256] * weight, own_field[256:] * weight], axis=0))
    exchange(send.at[0], recv.at[0], 2)
    gather_first(2, 0)
    gather_second(3)
    gather_first(2, 1)
    gather_second(4)
    gather_first(3, 0)
    gather_first(3, 1)
    exchanged(recv.at[0], 2)
    source = pick(recv[0])
    gather_last()

    def round_pair(k, carry):
        rows = pl.ds(pl.multiple_of(16 * k, 16), 16)
        high, low = split(gath[k // 16, (k // 4) % 4, pl.ds(pl.multiple_of(16 * (k % 4), 16), 16), :])
        gath_hi[rows, :] = high
        gath_lo[rows, :] = low
        return carry

    lax.fori_loop(0, 32, round_pair, 0)
    correlate(source, 0)
    across_chip(0, 3)
    across_ring(0, 4, 3)
    share(0, half_sum(0, 4), 6)
    direction = expand(shared(0, 6)) - source

    send[1] = spread(direction, PERTS)
    exchange(send.at[1], recv.at[1], 5)
    correlate(direction, 1)
    across_chip(1, 8)
    across_ring(1, 11, 8)
    exchanged(recv.at[1], 5)
    field[0] = to_planes(recv[1], y_hi, y_lo)
    local = jnp.concatenate([pot[...], pot[...]], axis=1)
    send[2] = from_planes(jnp.concatenate([field[0, :256] * local, field[0, 256:] * local], axis=0))
    exchange(send.at[2], recv.at[2], 7)
    corr_dir = half_sum(1, 11)
    share(1, corr_dir, 14)
    image = diag * direction + 2.0 * expand(shared(1, 14))
    exchanged(recv.at[2], 7)
    image = image + pick(recv[2])

    send[3] = spread(image, PERTS)
    exchange(send.at[3], recv.at[3], 9)
    lane = lax.broadcasted_iota(jnp.int32, (8, 128), 1)
    dots = jnp.where(lane == 0, over_lanes(direction * direction), 0.0)
    dots = jnp.where(lane == 1, over_lanes(direction * image), dots)
    dots = jnp.where(lane == 2, over_lanes(image * image), dots)
    sums(0, dots, 10)
    correlate(image, 2)
    across_chip(2, 15)
    across_ring(2, 16, 15)
    exchanged(recv.at[3], 9)
    field[1] = to_planes(recv[3], y_hi, y_lo)
    dots = summed(0, 10)
    norm = dots[:, 0:1]
    step0 = norm / dots[:, 1:2]
    norm_next = step0 * step0 * dots[:, 2:3] - norm
    grow = 1.0 + norm_next / norm
    direction1 = grow * direction - step0 * image
    field[1] = per_lane(grow) * field[0] - per_lane(step0) * field[1]
    corr_dir1 = grow * corr_dir - step0 * half_sum(2, 16)

    energy_terms = over_lanes(diag * direction1 * direction1)
    corr_terms = over_lanes(jnp.sum(corr_dir1 * corr_dir1, axis=0))
    corr_terms = corr_terms + pltpu.roll(jnp.broadcast_to(corr_terms, (8, 128)), 4, 0)[:, 0:1]
    energy_terms = energy_terms + corr_terms * (2.0 / (2.0 * NPW) / 8.0)
    real, imag = field[1, :256], field[1, 256:]
    squares = jnp.sum(local * (real * real + imag * imag), axis=0, keepdims=True)
    for p in range(PERTS):
        piece = over_lanes(squares[:, 64 * p : 64 * p + 64])
        energy_terms = energy_terms + jnp.where((sub8 % 4) == p, piece, 0.0)
    sums(1, jnp.broadcast_to(energy_terms, (8, 128)), 12)
    own_re, own_im = own_field[:256], own_field[256:]
    dens0 = own_re * field[0, :256] + own_im * field[0, 256:]
    dens1 = own_re * real + own_im * imag
    dens0 = 2.0 * per_lane(step0) * dens0
    step1 = norm_next / summed(1, 12)[:, 0:1]
    den_send[...] = dens0 + 2.0 * per_lane(step1) * dens1

    def give_density(k, carry):
        peer = band_peer(k)
        pltpu.make_async_remote_copy(
            src_ref=den_send.at[pl.ds(pl.multiple_of(8 * peer, 8), 8)],
            dst_ref=den_recv.at[pl.ds(pl.multiple_of(8 * r, 8), 8)],
            send_sem=ssem.at[13], recv_sem=rsem.at[13],
            device_id={"band": peer}, device_id_type=MESH,
        ).start()
        return carry

    lax.fori_loop(0, BANDS - 1, give_density, 0)
    sent.append((den_send.at[pl.ds(0, 8 * (BANDS - 1))], ssem.at[13]))
    here = pl.ds(pl.multiple_of(8 * r, 8), 8)
    den_recv[here, :] = den_send[here, :]
    response = step0 * direction + step1 * direction1
    for ri in range(2):
        dpsi[0, :, ri, :] = response[:PERTS, NJ * ri : NJ * ri + NJ]

    drain()
    drain_own()

    taken(den_recv.at[pl.ds(0, 8 * (BANDS - 1))], rsem.at[13])
    total = jnp.zeros((8, 256), F32)
    for k in range(BANDS):
        total = total + den_recv[8 * k : 8 * k + 8, :]
    for p in range(PERTS):
        for half in range(2):
            dens[p, :, 64 * half : 64 * half + 64] = total[4 * half : 4 * half + 4, 64 * p : 64 * p + 64]


def on_device(sphere_index, occupied, energies, local_pot, trial_pot):
    tables = [jnp.asarray(table) for table in make_tables()]
    vmem = pl.BlockSpec(memory_space=pltpu.VMEM)
    scratch = [pltpu.VMEM(table.shape, F32) for table in tables[2:]]
    scratch += [pltpu.VMEM(table.shape, BF16) for table in tables[2:] for _ in range(2)]
    scratch += [
        pltpu.VMEM((2, XS, 64, 2 * NJ), F32),
        pltpu.VMEM((512, 2 * NJ), BF16),
        pltpu.VMEM((512, 2 * NJ), BF16),
        pltpu.VMEM((2, NJ), F32),
        pltpu.VMEM((128, 2 * NJ), BF16),
        pltpu.VMEM((128, 2 * NJ), BF16),
        pltpu.VMEM((64, 2 * NJ), F32),
        pltpu.VMEM((256, 2 * NJ), BF16),
        pltpu.VMEM((256, 2 * NJ), BF16),
        pltpu.VMEM((128, 128), F32),
        pltpu.VMEM((128, 128), F32),
        pltpu.VMEM((4, 128, 256), F32),
        pltpu.VMEM((4, 128, 256), F32),
        pltpu.VMEM((3, 4, 8, 128), F32),
        pltpu.VMEM((3, 2, 8, 128), F32),
        pltpu.VMEM((3, 2, 8, 128), F32),
        pltpu.VMEM((3, 8, 2, 8, 128), F32),
        pltpu.VMEM((2, 4, 8, 128), F32),
        pltpu.VMEM((2, 8, 128), F32),
        pltpu.VMEM((2, GRID, 8, 128), F32),
        pltpu.VMEM((256, 256), F32),
        pltpu.VMEM((256, 256), F32),
        pltpu.VMEM((512, 256), F32),
        pltpu.VMEM((2, 512, 256), F32),
        pltpu.VMEM((256, 128), F32),
        pltpu.VMEM((256, 256), F32),
        pltpu.SemaphoreType.DMA((17,)),
        pltpu.SemaphoreType.DMA((17,)),
        pltpu.SemaphoreType.DMA((4,)),
        pltpu.SemaphoreType.DMA((23,)),
        pltpu.SemaphoreType.DMA((5,)),
    ]
    return pl.pallas_call(
        kernel,
        out_shape=(
            jax.ShapeDtypeStruct((1, PERTS, 2, NJ), F32),
            jax.ShapeDtypeStruct((PERTS, 4, 128), F32),
        ),
        in_specs=[vmem] * 7 + [pl.BlockSpec(memory_space=pl.ANY)] * 5,
        out_specs=(vmem, vmem),
        scratch_shapes=scratch,
        compiler_params=pltpu.CompilerParams(
            collective_id=0, has_side_effects=True, vmem_limit_bytes=60 * 1024 * 1024
        ),
        name="response",
    )(sphere_index, occupied, energies, local_pot, trial_pot, *tables)


def solution(mesh):
    return jax.shard_map(
        on_device,
        mesh=mesh,
        in_specs=(
            P("grid"),
            P("band", None, "grid"),
            P("band"),
            P("grid", None),
            P(None, "grid", None),
        ),
        out_specs=(P("band", None, None, "grid"), P(None, "grid", "band")),
        check_vma=False,
    )
```

```python
import numpy as np
import jax
import jax.numpy as jnp
import ml_dtypes
from jax import lax
from jax.experimental import pallas as pl
from jax.experimental.pallas import tpu as pltpu
from jax.sharding import PartitionSpec as P

NG = 64
NPW = 12288
NJ = 768
PERTS = 4
GRID = 16
XS, ZS = 4, 8
CUT = 640
BANDS = 32
KIN_SCALE = 0.02
MESH = pl.DeviceIdType.MESH
F32 = jnp.float32
BF16 = jnp.bfloat16


def halves(table):
    high = table.astype(ml_dtypes.bfloat16)
    low = (table - high.astype(np.float64)).astype(ml_dtypes.bfloat16)
    return high, low


def make_tables():
    freq = np.arange(32) - 32 * (np.arange(32) >= 16)
    norm = 1.0 / np.sqrt(NG)
    angle = 2 * np.pi / NG
    phase = np.exp(1j * angle * np.outer(np.arange(NG), freq)) * norm
    z_tab = np.zeros((NG, 2, 2, 32))
    for ri in range(2):
        value = phase * (1j**ri)
        z_tab[:, 0, ri], z_tab[:, 1, ri] = value.real, value.imag
    z_tab = z_tab.reshape(128, 64)
    y_tab = np.zeros((2, 2, 32, 2, 2, 2, NG))
    own_tab = np.zeros((2, 2, 32, 2, 2, 2, NG))
    for p in range(2):
        for k in range(2):
            y_tab[p, k, :, k, 0, p] = phase.real.T
            y_tab[p, k, :, k, 1, p] = phase.imag.T
            own_tab[0, k, :, k, 0, p] = phase.real.T
            own_tab[0, k, :, k, 1, p] = phase.imag.T
    y_tab = y_tab.reshape(128, 512)
    own_tab = own_tab.reshape(128, 512)
    x_tab = np.zeros((2, 32, 2, 4, 2, 2, GRID, 4, 2))
    for k in range(2):
        rotor = np.exp(1j * angle * np.outer(np.arange(NG), np.arange(GRID) - 16 * k)) * norm
        rotor = rotor.reshape(32, 2, GRID)
        for cs in range(2):
            for ri in range(2):
                value = rotor * (1j ** (cs + ri))
                for zl in range(4):
                    x_tab[0, :, :, zl, k, cs, :, zl, ri] = value.real
                    x_tab[1, :, :, zl, k, cs, :, zl, ri] = value.imag
    x_tab = x_tab.reshape(512, 512)
    return list(halves(z_tab)) + [t.astype(np.float32) for t in (own_tab, x_tab, y_tab, x_tab.T, y_tab.T)]


def split(value):
    high = value.astype(BF16)
    return high, (value - high.astype(F32)).astype(BF16)


def dot(a, b, ca, cb):
    return lax.dot_general(a, b, (((ca,), (cb,)), ((), ())), preferred_element_type=F32)


def dot3(a_high, a_low, b_high, b_low, ca=1, cb=0):
    total = dot(a_high, b_high, ca, cb) + dot(a_low, b_high, ca, cb)
    return total + dot(a_high, b_low, ca, cb)


def turn(vector):
    return jnp.concatenate([-vector[:, NJ:], vector[:, :NJ]], axis=1)


def kernel(
    sph, occ, energy, pot_in, trial_in, zt_hi, zt_lo, *refs,
):
    stored, (dpsi, dens), whole, kept, rest = refs[:5], refs[5:7], refs[7:12], refs[12:22], refs[22:]
    o_hi, o_lo, t_hi, t_lo, y_hi, y_lo, tt_hi, tt_lo, yt_hi, yt_lo = kept
    (
    gath_x, gath_z, gath_hi, gath_lo, own, ztab_hi, ztab_lo, col_mask, rhs_hi, rhs_lo,
    own_send, own_recv, send, recv, pair_send, pair_recv, half_send, half_recv, full_recv, sum_send, sum_recv,
    den_send, den_recv, coef_send, coef_recv, own_field, field, pot, trial, ssem, rsem, gsend, grecv, tsem,
    ) = rest
    g = lax.axis_index("grid")
    r = lax.axis_index("band")
    bx, bz = r // ZS, r % ZS
    gy, gc = g // 2, g % 2

    def ring(j, half):
        return half + (1 - 2 * (j % 2)) * ((j + 1) // 2)

    def grid_peer(k):
        return 2 * ((gy + ring(k // 2, 4)) % 8) + (gc + k + 1) % 2

    def band_peer(k):
        return ZS * ((bx + ring(k % 4, 2)) % XS) + (bz + ring(k // 4, 4)) % ZS

    barrier = pltpu.get_barrier_semaphore()

    def greet_grid(k, carry):
        pl.semaphore_signal(barrier, inc=1, device_id={"grid": grid_peer(k)}, device_id_type=MESH)
        return carry

    def greet_band(k, carry):
        pl.semaphore_signal(barrier, inc=1, device_id={"band": band_peer(k)}, device_id_type=MESH)
        return carry

    lax.fori_loop(0, BANDS - 1, greet_band, 0)
    lax.fori_loop(0, GRID - 1, greet_grid, 0)

    loads = [pltpu.make_async_copy(a, b, tsem.at[k]) for k, (a, b) in enumerate(zip(stored, whole))]
    for load in loads:
        load.start()

    def taken(ref, sem):
        pltpu.make_async_copy(ref, ref, sem).wait()

    sent = []

    def drain():
        for ref, sem in sent:
            taken(ref, sem)

    def to_band(src, dst, send_sem, recv_sem, x, z):
        pltpu.make_async_remote_copy(
            src_ref=src, dst_ref=dst, send_sem=send_sem, recv_sem=recv_sem,
            device_id={"band": x * ZS + z}, device_id_type=MESH,
        ).start()

    place = sph[...].reshape(1, NJ)
    kz, xl, ky = place // 256, (place // 64) % 4, place % 64
    kx = g + 16 * xl

    def wave(k):
        return jnp.where(k < 32, k, k - 64)

    fx, fy, fz = wave(kx), wave(ky), wave(kz)
    kinetic = KIN_SCALE * (fx * fx + fy * fy + fz * fz).astype(F32)
    diag = jnp.concatenate([kinetic, kinetic], axis=1) - energy[...].reshape(1, 1)
    one_z = jnp.where(lax.broadcasted_iota(jnp.int32, (32, NJ), 0) == (kz & 31), 1.0, 0.0).astype(BF16)
    column = (xl >> 1) * 32 + (ky & 31)
    one_col = jnp.where(lax.broadcasted_iota(jnp.int32, (64, NJ), 0) == column, 1.0, 0.0)
    col_mask[:, :NJ] = one_col
    col_mask[:, NJ:] = one_col
    for ri in range(2):
        lanes = pl.ds(ri * NJ, NJ)
        ztab_hi[:, lanes] = dot(zt_hi[:, 32 * ri : 32 * ri + 32], one_z, 1, 0).astype(BF16)
        ztab_lo[:, lanes] = dot(zt_lo[:, 32 * ri : 32 * ri + 32], one_z, 1, 0).astype(BF16)
    left = lax.broadcasted_iota(jnp.int32, (4, 128), 1) < 64

    def lay(t, carry):
        lanes = pl.ds(pl.multiple_of(128 * t, 128), 128)
        rows = pl.ds(pl.multiple_of(8 * t, 8), 8)
        for q in range(3):
            a, b = (pot_in[:, lanes],) * 2 if q == 2 else (trial_in[2 * q, :, lanes], trial_in[2 * q + 1, :, lanes])
            even = jnp.where(left, a, pltpu.roll(b, 64, 1))
            odd = jnp.where(left, pltpu.roll(a, 64, 1), b)
            both = jnp.concatenate([even, odd], axis=0)
            if q == 2:
                pot[rows, :] = both
            else:
                trial[rows, 128 * q : 128 * q + 128] = both
        return carry

    lax.fori_loop(0, 32, lay, 0)
    mine = jnp.concatenate([occ[:, 0, :], occ[:, 1, :]], axis=1)
    own_z = pl.ds(pl.multiple_of(16 * bz, 16), 16)
    gath_x[bx, own_z, :] = mine[:, :CUT]
    gath_z[bx, own_z, :] = mine[:, CUT:]

    for k, load in enumerate(loads):
        load.wait()
        for i in range(0, whole[k].shape[0], 64):
            high, low = split(whole[k][i : i + 64, :])
            kept[2 * k][i : i + 64, :] = high
            kept[2 * k + 1][i : i + 64, :] = low

    pl.semaphore_wait(barrier, GRID - 1 + BANDS - 1)

    @pl.when(r == 0)
    def _():
        pltpu.make_async_copy(occ.at[0], own, rsem.at[0]).start()

    @pl.when(r < 2)
    def _():
        def give(i, carry):
            pltpu.make_async_remote_copy(
                src_ref=occ.at[i], dst_ref=own, send_sem=ssem.at[0], recv_sem=rsem.at[0],
                device_id={"band": 16 * r + i}, device_id_type=MESH,
            ).start()
            return carry

        lax.fori_loop(jnp.where(r == 0, 1, 0), 16, give, 0)

    def drain_own():
        @pl.when(r == 0)
        def _():
            taken(occ.at[pl.ds(0, 15)], ssem.at[0])

        @pl.when(r == 1)
        def _():
            taken(occ, ssem.at[0])

    def block(part, x, z):
        return (gath_z if part else gath_x).at[x, pl.ds(pl.multiple_of(16 * z, 16), 16)]

    def col(z, first=0, count=XS):
        return gath_x.at[pl.ds(first, count), pl.ds(pl.multiple_of(16 * z, 16), 16)]

    z_up, z_dn = (bz + 1) % ZS, (bz + ZS - 1) % ZS

    def across(part, z, slot):
        for k in (2, 1, 3):
            to_band(block(part, bx, z), block(part, bx, z), gsend.at[slot], grecv.at[slot], (bx + k) % XS, bz)

    def below(d):
        return (bz + ZS - d) % ZS

    def above(d):
        return (bz + d) % ZS

    def first(way, d, half):
        return grecv.at[2 + 7 * way + (6 if d == 4 else 2 * d - 2 + half)]

    def second(way, d):
        return grecv.at[16 + 4 * way + d - 1]

    def send_first(way, z, d, half):
        ref = col(z, 2 * half, 2)
        to_band(ref, ref, gsend.at[2], first(way, d, half), bx, z_dn if way else z_up)

    def send_second(way, z, d):
        to_band(block(1, bx, z), block(1, bx, z), gsend.at[3], second(way, d), bx, z_dn if way else z_up)

    def gather_0():
        across(0, bz, 0)
        for way in range(2):
            send_second(way, bz, 1)
        across(1, bz, 1)
        sent.append((gath_x.at[pl.ds(0, 3), pl.ds(0, 16)], gsend.at[0]))
        sent.append((gath_z.at[pl.ds(0, 3)], gsend.at[1]))
        sent.append((gath_x.at[:, pl.ds(0, 112)], gsend.at[2]))
        sent.append((gath_z.at[0, pl.ds(0, 112)], gsend.at[3]))

    def gather_1():
        taken(gath_x.at[pl.ds(0, 3), pl.ds(0, 16)], grecv.at[0])
        for half in range(2):
            for way in range(2):
                send_first(way, bz, 1, half)

    def gather_first(d, half):
        for way in range(2):
            z = above(d) if way else below(d)
            if d < 3 or half == way:
                taken(col(z, 2 * half, 2), first(way, d, half))
                send_first(way, z, d + 1, half)

    def gather_second(d):
        for way in range(1 if d == 4 else 2):
            z = above(d) if way else below(d)
            taken(block(1, bx, z), second(way, d))
            if d + way < 4:
                send_second(way, z, d + 1)
            across(1, z, 1)

    def gather_last():
        taken(col(below(3), 2, 2), first(0, 3, 1))
        taken(col(above(3), 0, 2), first(1, 3, 0))
        taken(col(below(4), 0, 2), first(0, 4, 0))
        taken(col(below(4), 2, 2), first(1, 4, 1))
        taken(gath_z.at[pl.ds(0, 3)], grecv.at[1])

    def exchange(src, dst, slot):
        def go(k, carry):
            peer = grid_peer(k)
            pltpu.make_async_remote_copy(
                src_ref=src.at[pl.ds(pl.multiple_of(8 * peer, 8), 8)],
                dst_ref=dst.at[pl.ds(pl.multiple_of(8 * g, 8), 8)],
                send_sem=ssem.at[slot], recv_sem=rsem.at[slot],
                device_id={"grid": peer}, device_id_type=MESH,
            ).start()
            return carry

        lax.fori_loop(0, GRID - 1, go, 0)
        sent.append((src.at[pl.ds(0, 8 * (GRID - 1))], ssem.at[slot]))
        here = pl.ds(pl.multiple_of(8 * g, 8), 8)
        dst[here, :] = src[here, :]

    def exchanged(dst, slot):
        taken(dst.at[pl.ds(0, 8 * (GRID - 1))], rsem.at[slot])

    other = 1 - gc

    def to_other(src, dst, slot):
        pltpu.make_async_remote_copy(
            src_ref=src, dst_ref=dst, send_sem=ssem.at[slot], recv_sem=rsem.at[slot],
            device_id={"grid": 2 * gy + other}, device_id_type=MESH,
        ).start()
        sent.append((src, ssem.at[slot]))

    def across_chip(n, slot):
        to_other(pair_send.at[n, pl.ds(2 * other, 2)], pair_recv.at[n], slot)

    def across_ring(n, slot, slot_in):
        taken(pair_recv.at[n], rsem.at[slot_in])
        total = pair_send[n, pl.ds(2 * gc, 2)] + pair_recv[n]
        half_send[n] = total

        def go(k, carry):
            pltpu.make_async_remote_copy(
                src_ref=half_send.at[n], dst_ref=half_recv.at[n, gy],
                send_sem=ssem.at[slot], recv_sem=rsem.at[slot],
                device_id={"grid": 2 * ((gy + ring(k, 4)) % 8) + gc}, device_id_type=MESH,
            ).start()
            return carry

        lax.fori_loop(0, 7, go, 0)
        sent.append((half_recv.at[n, pl.ds(0, 7)], ssem.at[slot]))
        half_recv[n, gy] = total

    def half_sum(n, slot):
        taken(half_recv.at[n, pl.ds(0, 7)], rsem.at[slot])
        return jnp.sum(half_recv[n], axis=0)

    def share(n, total, slot):
        full_recv[n, pl.ds(2 * gc, 2)] = total
        to_other(full_recv.at[n, pl.ds(2 * gc, 2)], full_recv.at[n, pl.ds(2 * gc, 2)], slot)

    def shared(n, slot):
        taken(full_recv.at[n, pl.ds(0, 2)], rsem.at[slot])
        return jnp.concatenate([full_recv[n, k] for k in range(4)], axis=1)

    def sums(n, value, slot):
        sum_send[n] = value

        def go(k, carry):
            pltpu.make_async_remote_copy(
                src_ref=sum_send.at[n], dst_ref=sum_recv.at[n, g],
                send_sem=ssem.at[slot], recv_sem=rsem.at[slot],
                device_id={"grid": grid_peer(k)}, device_id_type=MESH,
            ).start()
            return carry

        lax.fori_loop(0, GRID - 1, go, 0)
        sent.append((sum_recv.at[n, pl.ds(0, GRID - 1)], ssem.at[slot]))
        sum_recv[n, g] = value

    def summed(n, slot):
        taken(sum_recv.at[n, pl.ds(0, GRID - 1)], rsem.at[slot])
        return jnp.sum(sum_recv[n], axis=0)

    def spread(rows):
        mask = col_mask[...]
        for p, row in enumerate(rows):
            high = row.astype(BF16).astype(F32)
            rhs_hi[64 * p : 64 * p + 64, :] = (mask * high).astype(BF16)
            rhs_lo[64 * p : 64 * p + 64, :] = (mask * (row - high)).astype(BF16)
        return dot3(ztab_hi[...], ztab_lo[...], rhs_hi[...], rhs_lo[...], 1, 1)

    def to_planes(spectral, yh, yl):
        high, low = split(spectral)
        part = dot3(high, low, yh[...], yl[...])
        part = jnp.concatenate([part[:, 128 * k : 128 * k + 128] for k in range(4)], axis=0)
        high, low = split(part)
        return dot3(t_hi[...], t_lo[...], high, low)

    def from_planes(values, factor):
        values = jnp.concatenate([values[:256] * factor, values[256:] * factor], axis=0)
        high, low = split(values)
        part = dot3(tt_hi[...], tt_lo[...], high, low)
        part = jnp.concatenate([part[128 * k : 128 * k + 128] for k in range(4)], axis=1)
        high, low = split(part)
        return dot3(high, low, yt_hi[...], yt_lo[...])

    sub8 = lax.broadcasted_iota(jnp.int32, (8, 1), 0)

    def pick(spectral, start, h):
        high, low = split(jnp.transpose(spectral))
        result = start
        for p in range(2):
            rows = slice(64 * p, 64 * p + 64)
            box = dot3(high[rows], low[rows], ztab_hi[...], ztab_lo[...])
            line = jnp.sum(box * col_mask[...], axis=0, keepdims=True)
            result = result + jnp.where(sub8 == 2 * h + p, line, 0.0)
            result = result + jnp.where(sub8 == 2 * h + p + 4, -turn(line), 0.0)
        return result

    def forward(vector, n, h):
        send[n, h] = spread([vector[2 * h + p : 2 * h + p + 1] for p in range(2)])
        exchange(send.at[n, h], recv.at[n, h], 17 + 2 * n + h)

    def arrived(n, h):
        exchanged(recv.at[n, h], 17 + 2 * n + h)
        return recv[n, h]

    def backward(values, factor, n, h):
        send[n, h] = from_planes(values, factor)
        exchange(send.at[n, h], recv.at[n, h], 17 + 2 * n + h)

    def correlate(vector, n):
        high = vector.astype(BF16).astype(F32)
        both = jnp.concatenate([high, vector - high], axis=0).astype(BF16)
        first = dot(both, gath_hi[...], 1, 1)
        second = dot(both, gath_lo[...], 1, 1)
        total = first[:8] + first[8:] + second[:8]
        for k in range(4):
            pair_send[n, k] = total[:, 128 * k : 128 * k + 128]

    sign = jnp.where(sub8 < 4, 1.0, -1.0)

    def expand(correlations):
        high = correlations.astype(BF16).astype(F32)
        both = jnp.concatenate([high, correlations - high], axis=0).astype(BF16)
        first = dot(both, gath_hi[...], 1, 0)
        second = dot(both, gath_lo[...], 1, 0)
        direct = first[:8] + first[8:] + second[:8]
        return (direct + sign * turn(pltpu.roll(direct, 4, 0))) * (1.0 / (2.0 * NPW))

    lane = lax.broadcasted_iota(jnp.int32, (1, 128), 1)

    def per_lane(column, h):
        return jnp.where(lane < 64, column[2 * h : 2 * h + 1], column[2 * h + 1 : 2 * h + 2])

    def as_row(columns):
        total = jnp.zeros((8, 128), F32)
        for k, column in enumerate(columns):
            total = total + jnp.where(lane == sub8 + 8 * k, column, 0.0)
        return jnp.sum(total, axis=0, keepdims=True)

    def as_column(row, k):
        return jnp.sum(jnp.where(lane == sub8 + 8 * k, row, 0.0), axis=1, keepdims=True)

    def over_lanes(value):
        return jnp.sum(value, axis=1, keepdims=True)

    def to_all_bands(src, dst, slot, rows):
        def go(k, carry):
            peer = band_peer(k)
            part = src if rows is None else src.at[pl.ds(pl.multiple_of(rows * peer, rows), rows)]
            place = dst.at[r] if rows is None else dst.at[pl.ds(pl.multiple_of(rows * r, rows), rows)]
            pltpu.make_async_remote_copy(
                src_ref=part, dst_ref=place, send_sem=ssem.at[slot], recv_sem=rsem.at[slot],
                device_id={"band": peer}, device_id_type=MESH,
            ).start()
            return carry

        lax.fori_loop(0, BANDS - 1, go, 0)

    def give_density(n, slot):
        to_all_bands(den_send.at[n], den_recv.at[n], slot, 8)
        sent.append((den_send.at[n, pl.ds(0, 8 * (BANDS - 1))], ssem.at[slot]))
        here = pl.ds(pl.multiple_of(8 * r, 8), 8)
        den_recv[n, here, :] = den_send[n, here, :]

    def overlap(n, h, real, imag):
        den_send[n, :, 128 * h : 128 * h + 128] = 2.0 * (own_field[:256] * real + own_field[256:] * imag)

    gather_0()
    taken(own, rsem.at[0])
    own_row = jnp.concatenate([own[0:1, :], own[1:2, :]], axis=1)
    own_send[...] = spread([own_row, own_row])
    exchange(own_send, own_recv, 1)
    gather_1()
    gather_second(1)
    gather_first(1, 0)
    gather_second(2)
    gather_first(1, 1)
    exchanged(own_recv, 1)
    own_field[...] = to_planes(own_recv[...], o_hi, o_lo)

    for h in range(2):
        backward(own_field[...], trial[:, 128 * h : 128 * h + 128], 0, h)
    gather_first(2, 0)
    gather_second(3)
    gather_first(2, 1)
    gather_second(4)
    gather_first(3, 0)
    gather_first(3, 1)
    source = pick(arrived(0, 0), jnp.zeros((8, 2 * NJ), F32), 0)
    source = pick(arrived(0, 1), source, 1)
    gather_last()

    def round_pair(k, carry):
        rows = pl.ds(pl.multiple_of(16 * k, 16), 16)
        from_rows = pl.ds(pl.multiple_of(16 * (k % ZS), 16), 16)
        gath_hi[rows, :CUT], gath_lo[rows, :CUT] = split(gath_x[k // ZS, from_rows, :])
        gath_hi[rows, CUT:], gath_lo[rows, CUT:] = split(gath_z[k // ZS, from_rows, :])
        return carry

    lax.fori_loop(0, 32, round_pair, 0)
    correlate(source, 0)
    across_chip(0, 3)
    across_ring(0, 4, 3)
    share(0, half_sum(0, 4), 6)
    direction = expand(shared(0, 6)) - source

    for h in range(2):
        forward(direction, 1, h)
    correlate(direction, 1)
    across_chip(1, 8)
    across_ring(1, 11, 8)
    local = pot[...]
    for h in range(2):
        field[0, h] = to_planes(arrived(1, h), y_hi, y_lo)
        backward(field[0, h], local, 2, h)
    corr_dir = half_sum(1, 11)
    share(1, corr_dir, 14)
    for h in range(2):
        overlap(0, h, field[0, h, :256], field[0, h, 256:])
    give_density(0, 13)
    image = diag * direction + 2.0 * expand(shared(1, 14))

    for h in range(2):
        image = pick(arrived(2, h), image, h)
        forward(image, 3, h)
    dots = [over_lanes(direction * direction), over_lanes(direction * image), over_lanes(image * image)]
    sums(0, as_row(dots), 10)
    correlate(image, 2)
    across_chip(2, 15)
    across_ring(2, 16, 15)
    for h in range(2):
        field[1, h] = to_planes(arrived(3, h), y_hi, y_lo)
        overlap(1, h, field[1, h, :256], field[1, h, 256:])
    give_density(1, 9)
    dots = summed(0, 10)
    norm, curve, square = (as_column(dots, k) for k in range(3))
    step0 = norm / curve
    norm_next = step0 * step0 * square - norm
    grow = 1.0 + norm_next / norm
    direction1 = grow * direction - step0 * image
    corr_dir1 = grow * corr_dir - step0 * half_sum(2, 16)

    terms = over_lanes(diag * direction1 * direction1)
    corr_terms = over_lanes(jnp.sum(corr_dir1 * corr_dir1, axis=0))
    corr_terms = corr_terms + pltpu.roll(jnp.broadcast_to(corr_terms, (8, 128)), 4, 0)[:, 0:1]
    terms = terms + corr_terms * (2.0 / (2.0 * NPW) / 8.0)
    for h in range(2):
        mixed = per_lane(grow, h) * field[0, h] - per_lane(step0, h) * field[1, h]
        real, imag = mixed[:256], mixed[256:]
        squares = jnp.sum(local * (real * real + imag * imag), axis=0, keepdims=True)
        for p in range(2):
            piece = over_lanes(squares[:, 64 * p : 64 * p + 64])
            terms = terms + jnp.where((sub8 % 4) == 2 * h + p, piece, 0.0)
    sums(1, as_row([terms]), 12)
    step1 = norm_next / as_column(summed(1, 12), 0)
    weights = (step0 + step1 * grow, -(step1 * step0))
    for n in range(2):
        for h in range(2):
            coef_send[2 * n + h : 2 * n + h + 1, :] = per_lane(weights[n], h)
    to_all_bands(coef_send, coef_recv, 5, None)
    sent.append((coef_recv.at[pl.ds(0, BANDS - 1)], ssem.at[5]))
    coef_recv[r] = coef_send[...]
    response = step0 * direction + step1 * direction1
    for ri in range(2):
        dpsi[0, :, ri, :] = response[:PERTS, NJ * ri : NJ * ri + NJ]

    drain()
    drain_own()

    for n, slot in ((0, 13), (1, 9)):
        taken(den_recv.at[n, pl.ds(0, 8 * (BANDS - 1))], rsem.at[slot])
    taken(coef_recv.at[pl.ds(0, BANDS - 1)], rsem.at[5])
    for h in range(2):
        total = jnp.zeros((8, 128), F32)
        for k in range(BANDS):
            for n in range(2):
                piece = den_recv[n, 8 * k : 8 * k + 8, 128 * h : 128 * h + 128]
                total = total + coef_recv[k, 2 * n + h : 2 * n + h + 1, :] * piece
        for p in range(2):
            for half in range(2):
                piece = total[4 * half : 4 * half + 4, 64 * p : 64 * p + 64]
                dens[2 * h + p, :, 64 * half : 64 * half + 64] = piece


def on_device(sphere_index, occupied, energies, local_pot, trial_pot):
    tables = [jnp.asarray(table) for table in make_tables()]
    vmem = pl.BlockSpec(memory_space=pltpu.VMEM)
    scratch = [pltpu.VMEM(table.shape, F32) for table in tables[2:]]
    scratch += [pltpu.VMEM(table.shape, BF16) for table in tables[2:] for _ in range(2)]
    scratch += [
        pltpu.VMEM((XS, 128, CUT), F32),
        pltpu.VMEM((XS, 128, 2 * NJ - CUT), F32),
        pltpu.VMEM((512, 2 * NJ), BF16),
        pltpu.VMEM((512, 2 * NJ), BF16),
        pltpu.VMEM((2, NJ), F32),
        pltpu.VMEM((128, 2 * NJ), BF16),
        pltpu.VMEM((128, 2 * NJ), BF16),
        pltpu.VMEM((64, 2 * NJ), F32),
        pltpu.VMEM((128, 2 * NJ), BF16),
        pltpu.VMEM((128, 2 * NJ), BF16),
        pltpu.VMEM((128, 128), F32),
        pltpu.VMEM((128, 128), F32),
        pltpu.VMEM((4, 2, 128, 128), F32),
        pltpu.VMEM((4, 2, 128, 128), F32),
        pltpu.VMEM((3, 4, 8, 128), F32),
        pltpu.VMEM((3, 2, 8, 128), F32),
        pltpu.VMEM((3, 2, 8, 128), F32),
        pltpu.VMEM((3, 8, 2, 8, 128), F32),
        pltpu.VMEM((2, 4, 8, 128), F32),
        pltpu.VMEM((2, 1, 128), F32),
        pltpu.VMEM((2, GRID, 1, 128), F32),
        pltpu.VMEM((2, 256, 256), F32),
        pltpu.VMEM((2, 256, 256), F32),
        pltpu.VMEM((4, 128), F32),
        pltpu.VMEM((BANDS, 4, 128), F32),
        pltpu.VMEM((512, 128), F32),
        pltpu.VMEM((2, 2, 512, 128), F32),
        pltpu.VMEM((256, 128), F32),
        pltpu.VMEM((256, 256), F32),
        pltpu.SemaphoreType.DMA((25,)),
        pltpu.SemaphoreType.DMA((25,)),
        pltpu.SemaphoreType.DMA((4,)),
        pltpu.SemaphoreType.DMA((23,)),
        pltpu.SemaphoreType.DMA((5,)),
    ]
    return pl.pallas_call(
        kernel,
        out_shape=(
            jax.ShapeDtypeStruct((1, PERTS, 2, NJ), F32),
            jax.ShapeDtypeStruct((PERTS, 4, 128), F32),
        ),
        in_specs=[vmem] * 7 + [pl.BlockSpec(memory_space=pl.ANY)] * 5,
        out_specs=(vmem, vmem),
        scratch_shapes=scratch,
        compiler_params=pltpu.CompilerParams(
            collective_id=0, has_side_effects=True, vmem_limit_bytes=60 * 1024 * 1024
        ),
        name="response",
    )(sphere_index, occupied, energies, local_pot, trial_pot, *tables)


def solution(mesh):
    return jax.shard_map(
        on_device,
        mesh=mesh,
        in_specs=(
            P("grid"),
            P("band", None, "grid"),
            P("band"),
            P("grid", None),
            P(None, "grid", None),
        ),
        out_specs=(P("band", None, None, "grid"), P(None, "grid", "band")),
        check_vma=False,
    )
```

```python
import numpy as np
import jax
import jax.numpy as jnp
import ml_dtypes
from jax import lax
from jax.experimental import pallas as pl
from jax.experimental.pallas import tpu as pltpu
from jax.sharding import PartitionSpec as P

NG = 64
NPW = 12288
NJ = 768
PERTS = 4
GRID = 16
XS, ZS = 4, 8
CUT = 640
BANDS = 32
KIN_SCALE = 0.02
MESH = pl.DeviceIdType.MESH
F32 = jnp.float32
BF16 = jnp.bfloat16


def halves(table):
    high = table.astype(ml_dtypes.bfloat16)
    low = (table - high.astype(np.float64)).astype(ml_dtypes.bfloat16)
    return high, low


def make_tables():
    freq = np.arange(32) - 32 * (np.arange(32) >= 16)
    norm = 1.0 / np.sqrt(NG)
    angle = 2 * np.pi / NG
    phase = np.exp(1j * angle * np.outer(np.arange(NG), freq)) * norm
    z_tab = np.zeros((NG, 2, 2, 32))
    for ri in range(2):
        value = phase * (1j**ri)
        z_tab[:, 0, ri], z_tab[:, 1, ri] = value.real, value.imag
    z_tab = z_tab.reshape(128, 64)
    y_tab = np.zeros((2, 2, 32, 2, 2, 2, NG))
    own_tab = np.zeros((2, 2, 32, 2, 2, 2, NG))
    for p in range(2):
        for k in range(2):
            y_tab[p, k, :, k, 0, p] = phase.real.T
            y_tab[p, k, :, k, 1, p] = phase.imag.T
            own_tab[0, k, :, k, 0, p] = phase.real.T
            own_tab[0, k, :, k, 1, p] = phase.imag.T
    y_tab = y_tab.reshape(128, 512)
    own_tab = own_tab.reshape(128, 512)
    x_tab = np.zeros((2, 32, 2, 4, 2, 2, GRID, 4, 2))
    for k in range(2):
        rotor = np.exp(1j * angle * np.outer(np.arange(NG), np.arange(GRID) - 16 * k)) * norm
        rotor = rotor.reshape(32, 2, GRID)
        for cs in range(2):
            for ri in range(2):
                value = rotor * (1j ** (cs + ri))
                for zl in range(4):
                    x_tab[0, :, :, zl, k, cs, :, zl, ri] = value.real
                    x_tab[1, :, :, zl, k, cs, :, zl, ri] = value.imag
    x_tab = x_tab.reshape(512, 512)
    return list(halves(z_tab)) + [t.astype(np.float32) for t in (own_tab, x_tab, y_tab, x_tab.T, y_tab.T)]


def split(value):
    high = value.astype(BF16)
    return high, (value - high.astype(F32)).astype(BF16)


def dot(a, b, ca, cb):
    return lax.dot_general(a, b, (((ca,), (cb,)), ((), ())), preferred_element_type=F32)


def dot3(a_high, a_low, b_high, b_low, ca=1, cb=0):
    total = dot(a_high, b_high, ca, cb) + dot(a_low, b_high, ca, cb)
    return total + dot(a_high, b_low, ca, cb)


def turn(vector):
    return jnp.concatenate([-vector[:, NJ:], vector[:, :NJ]], axis=1)


def kernel(
    sph, occ_hbm, energy, pot_hbm, trial_hbm, zt_hi, zt_lo, *refs,
):
    stored, (dpsi, dens), whole, kept, rest = refs[:5], refs[5:7], refs[7:12], refs[12:22], refs[22:]
    o_hi, o_lo, t_hi, t_lo, y_hi, y_lo, tt_hi, tt_lo, yt_hi, yt_lo = kept
    (
    gath_x, gath_z, gath_hi, gath_lo, own, ztab_hi, ztab_lo, col_mask, rhs_hi, rhs_lo,
    own_send, own_recv, send, recv, pair_send, pair_recv, half_send, half_recv, full_recv, sum_send, sum_recv,
    den_send, den_recv, coef_send, coef_recv, own_field, field, pot, trial, occ, pot_in, trial_in, ssem, rsem, gsend, grecv, tsem,
    ) = rest
    g = lax.axis_index("grid")
    r = lax.axis_index("band")
    bx, bz = r // ZS, r % ZS
    gy, gc = g // 2, g % 2

    def ring(j, half):
        return half + (1 - 2 * (j % 2)) * ((j + 1) // 2)

    def grid_peer(k):
        return 2 * ((gy + ring(k // 2, 4)) % 8) + (gc + k + 1) % 2

    def band_peer(k):
        return ZS * ((bx + ring(k % 4, 2)) % XS) + (bz + ring(k // 4, 4)) % ZS

    barrier = pltpu.get_barrier_semaphore()

    def greet_grid(k, carry):
        pl.semaphore_signal(barrier, inc=1, device_id={"grid": grid_peer(k)}, device_id_type=MESH)
        return carry

    def greet_band(k, carry):
        pl.semaphore_signal(barrier, inc=1, device_id={"band": band_peer(k)}, device_id_type=MESH)
        return carry

    lax.fori_loop(0, BANDS - 1, greet_band, 0)
    lax.fori_loop(0, GRID - 1, greet_grid, 0)

    loads = [pltpu.make_async_copy(a, b, tsem.at[k]) for k, (a, b) in enumerate(zip(stored, whole))]
    inputs = ((occ_hbm, occ), (pot_hbm, pot_in), (trial_hbm, trial_in))
    inputs = [pltpu.make_async_copy(a, b, tsem.at[5 + k]) for k, (a, b) in enumerate(inputs)]
    for load in inputs + loads:
        load.start()

    def taken(ref, sem):
        pltpu.make_async_copy(ref, ref, sem).wait()

    sent = []

    def drain():
        for ref, sem in sent:
            taken(ref, sem)

    def to_band(src, dst, send_sem, recv_sem, x, z):
        pltpu.make_async_remote_copy(
            src_ref=src, dst_ref=dst, send_sem=send_sem, recv_sem=recv_sem,
            device_id={"band": x * ZS + z}, device_id_type=MESH,
        ).start()

    place = sph[...].reshape(1, NJ)
    kz, xl, ky = place // 256, (place // 64) % 4, place % 64
    kx = g + 16 * xl

    def wave(k):
        return jnp.where(k < 32, k, k - 64)

    fx, fy, fz = wave(kx), wave(ky), wave(kz)
    kinetic = KIN_SCALE * (fx * fx + fy * fy + fz * fz).astype(F32)
    diag = jnp.concatenate([kinetic, kinetic], axis=1) - energy[...].reshape(1, 1)
    one_z = jnp.where(lax.broadcasted_iota(jnp.int32, (32, NJ), 0) == (kz & 31), 1.0, 0.0).astype(BF16)
    column = (xl >> 1) * 32 + (ky & 31)
    one_col = jnp.where(lax.broadcasted_iota(jnp.int32, (64, NJ), 0) == column, 1.0, 0.0)
    col_mask[:, :NJ] = one_col
    col_mask[:, NJ:] = one_col
    for ri in range(2):
        lanes = pl.ds(ri * NJ, NJ)
        ztab_hi[:, lanes] = dot(zt_hi[:, 32 * ri : 32 * ri + 32], one_z, 1, 0).astype(BF16)
        ztab_lo[:, lanes] = dot(zt_lo[:, 32 * ri : 32 * ri + 32], one_z, 1, 0).astype(BF16)
    for load in inputs:
        load.wait()

    left = lax.broadcasted_iota(jnp.int32, (4, 128), 1) < 64

    def lay(t, carry):
        lanes = pl.ds(pl.multiple_of(128 * t, 128), 128)
        rows = pl.ds(pl.multiple_of(8 * t, 8), 8)
        for q in range(3):
            a, b = (pot_in[:, lanes],) * 2 if q == 2 else (trial_in[2 * q, :, lanes], trial_in[2 * q + 1, :, lanes])
            even = jnp.where(left, a, pltpu.roll(b, 64, 1))
            odd = jnp.where(left, pltpu.roll(a, 64, 1), b)
            both = jnp.concatenate([even, odd], axis=0)
            if q == 2:
                pot[rows, :] = both
            else:
                trial[rows, 128 * q : 128 * q + 128] = both
        return carry

    lax.fori_loop(0, 32, lay, 0)
    mine = jnp.concatenate([occ[:, 0, :], occ[:, 1, :]], axis=1)
    own_z = pl.ds(pl.multiple_of(16 * bz, 16), 16)
    gath_x[bx, own_z, :] = mine[:, :CUT]
    gath_z[bx, own_z, :] = mine[:, CUT:]

    for k, load in enumerate(loads):
        load.wait()
        for i in range(0, whole[k].shape[0], 64):
            high, low = split(whole[k][i : i + 64, :])
            kept[2 * k][i : i + 64, :] = high
            kept[2 * k + 1][i : i + 64, :] = low

    pl.semaphore_wait(barrier, GRID - 1 + BANDS - 1)

    @pl.when(r == 0)
    def _():
        pltpu.make_async_copy(occ.at[0], own, rsem.at[0]).start()

    @pl.when(r < 2)
    def _():
        def give(i, carry):
            pltpu.make_async_remote_copy(
                src_ref=occ.at[i], dst_ref=own, send_sem=ssem.at[0], recv_sem=rsem.at[0],
                device_id={"band": 16 * r + i}, device_id_type=MESH,
            ).start()
            return carry

        lax.fori_loop(jnp.where(r == 0, 1, 0), 16, give, 0)

    def drain_own():
        @pl.when(r == 0)
        def _():
            taken(occ.at[pl.ds(0, 15)], ssem.at[0])

        @pl.when(r == 1)
        def _():
            taken(occ, ssem.at[0])

    def block(part, x, z):
        return (gath_z if part else gath_x).at[x, pl.ds(pl.multiple_of(16 * z, 16), 16)]

    def col(z, first=0, count=XS):
        return gath_x.at[pl.ds(first, count), pl.ds(pl.multiple_of(16 * z, 16), 16)]

    z_up, z_dn = (bz + 1) % ZS, (bz + ZS - 1) % ZS

    def across(part, z, slot):
        for k in (2, 1, 3):
            to_band(block(part, bx, z), block(part, bx, z), gsend.at[slot], grecv.at[slot], (bx + k) % XS, bz)

    def below(d):
        return (bz + ZS - d) % ZS

    def above(d):
        return (bz + d) % ZS

    def first(way, d, half):
        return grecv.at[2 + 7 * way + (6 if d == 4 else 2 * d - 2 + half)]

    def second(way, d):
        return grecv.at[16 + 4 * way + d - 1]

    def send_first(way, z, d, half):
        ref = col(z, 2 * half, 2)
        to_band(ref, ref, gsend.at[2], first(way, d, half), bx, z_dn if way else z_up)

    def send_second(way, z, d):
        to_band(block(1, bx, z), block(1, bx, z), gsend.at[3], second(way, d), bx, z_dn if way else z_up)

    def gather_0():
        across(0, bz, 0)
        for way in range(2):
            send_second(way, bz, 1)
        across(1, bz, 1)
        sent.append((gath_x.at[pl.ds(0, 3), pl.ds(0, 16)], gsend.at[0]))
        sent.append((gath_z.at[pl.ds(0, 3)], gsend.at[1]))
        sent.append((gath_x.at[:, pl.ds(0, 112)], gsend.at[2]))
        sent.append((gath_z.at[0, pl.ds(0, 112)], gsend.at[3]))

    def gather_1():
        taken(gath_x.at[pl.ds(0, 3), pl.ds(0, 16)], grecv.at[0])
        for half in range(2):
            for way in range(2):
                send_first(way, bz, 1, half)

    def gather_first(d, half):
        for way in range(2):
            z = above(d) if way else below(d)
            if d < 3 or half == way:
                taken(col(z, 2 * half, 2), first(way, d, half))
                send_first(way, z, d + 1, half)

    def gather_second(d):
        for way in range(1 if d == 4 else 2):
            z = above(d) if way else below(d)
            taken(block(1, bx, z), second(way, d))
            if d + way < 4:
                send_second(way, z, d + 1)
            across(1, z, 1)

    def gather_last():
        taken(col(below(3), 2, 2), first(0, 3, 1))
        taken(col(above(3), 0, 2), first(1, 3, 0))
        taken(col(below(4), 0, 2), first(0, 4, 0))
        taken(col(below(4), 2, 2), first(1, 4, 1))
        taken(gath_z.at[pl.ds(0, 3)], grecv.at[1])

    def exchange(src, dst, slot):
        def go(k, carry):
            peer = grid_peer(k)
            pltpu.make_async_remote_copy(
                src_ref=src.at[pl.ds(pl.multiple_of(8 * peer, 8), 8)],
                dst_ref=dst.at[pl.ds(pl.multiple_of(8 * g, 8), 8)],
                send_sem=ssem.at[slot], recv_sem=rsem.at[slot],
                device_id={"grid": peer}, device_id_type=MESH,
            ).start()
            return carry

        lax.fori_loop(0, GRID - 1, go, 0)
        sent.append((src.at[pl.ds(0, 8 * (GRID - 1))], ssem.at[slot]))
        here = pl.ds(pl.multiple_of(8 * g, 8), 8)
        dst[here, :] = src[here, :]

    def exchanged(dst, slot):
        taken(dst.at[pl.ds(0, 8 * (GRID - 1))], rsem.at[slot])

    other = 1 - gc

    def to_other(src, dst, slot):
        pltpu.make_async_remote_copy(
            src_ref=src, dst_ref=dst, send_sem=ssem.at[slot], recv_sem=rsem.at[slot],
            device_id={"grid": 2 * gy + other}, device_id_type=MESH,
        ).start()
        sent.append((src, ssem.at[slot]))

    def across_chip(n, slot):
        to_other(pair_send.at[n, pl.ds(2 * other, 2)], pair_recv.at[n], slot)

    def across_ring(n, slot, slot_in):
        taken(pair_recv.at[n], rsem.at[slot_in])
        total = pair_send[n, pl.ds(2 * gc, 2)] + pair_recv[n]
        half_send[n] = total

        def go(k, carry):
            pltpu.make_async_remote_copy(
                src_ref=half_send.at[n], dst_ref=half_recv.at[n, gy],
                send_sem=ssem.at[slot], recv_sem=rsem.at[slot],
                device_id={"grid": 2 * ((gy + ring(k, 4)) % 8) + gc}, device_id_type=MESH,
            ).start()
            return carry

        lax.fori_loop(0, 7, go, 0)
        sent.append((half_recv.at[n, pl.ds(0, 7)], ssem.at[slot]))
        half_recv[n, gy] = total

    def half_sum(n, slot):
        taken(half_recv.at[n, pl.ds(0, 7)], rsem.at[slot])
        return jnp.sum(half_recv[n], axis=0)

    def share(n, total, slot):
        full_recv[n, pl.ds(2 * gc, 2)] = total
        to_other(full_recv.at[n, pl.ds(2 * gc, 2)], full_recv.at[n, pl.ds(2 * gc, 2)], slot)

    def shared(n, slot):
        taken(full_recv.at[n, pl.ds(0, 2)], rsem.at[slot])
        return jnp.concatenate([full_recv[n, k] for k in range(4)], axis=1)

    def sums(n, value, slot):
        sum_send[n] = value

        def go(k, carry):
            pltpu.make_async_remote_copy(
                src_ref=sum_send.at[n], dst_ref=sum_recv.at[n, g],
                send_sem=ssem.at[slot], recv_sem=rsem.at[slot],
                device_id={"grid": grid_peer(k)}, device_id_type=MESH,
            ).start()
            return carry

        lax.fori_loop(0, GRID - 1, go, 0)
        sent.append((sum_recv.at[n, pl.ds(0, GRID - 1)], ssem.at[slot]))
        sum_recv[n, g] = value

    def summed(n, slot):
        taken(sum_recv.at[n, pl.ds(0, GRID - 1)], rsem.at[slot])
        return jnp.sum(sum_recv[n], axis=0)

    def spread(rows):
        mask = col_mask[...]
        for p, row in enumerate(rows):
            high = row.astype(BF16).astype(F32)
            rhs_hi[64 * p : 64 * p + 64, :] = (mask * high).astype(BF16)
            rhs_lo[64 * p : 64 * p + 64, :] = (mask * (row - high)).astype(BF16)
        return dot3(ztab_hi[...], ztab_lo[...], rhs_hi[...], rhs_lo[...], 1, 1)

    def to_planes(spectral, yh, yl):
        high, low = split(spectral)
        part = dot3(high, low, yh[...], yl[...])
        part = jnp.concatenate([part[:, 128 * k : 128 * k + 128] for k in range(4)], axis=0)
        high, low = split(part)
        return dot3(t_hi[...], t_lo[...], high, low)

    def from_planes(values, factor):
        values = jnp.concatenate([values[:256] * factor, values[256:] * factor], axis=0)
        high, low = split(values)
        part = dot3(tt_hi[...], tt_lo[...], high, low)
        part = jnp.concatenate([part[128 * k : 128 * k + 128] for k in range(4)], axis=1)
        high, low = split(part)
        return dot3(high, low, yt_hi[...], yt_lo[...])

    sub8 = lax.broadcasted_iota(jnp.int32, (8, 1), 0)

    def pick(spectral, start, h):
        high, low = split(jnp.transpose(spectral))
        result = start
        for p in range(2):
            rows = slice(64 * p, 64 * p + 64)
            box = dot3(high[rows], low[rows], ztab_hi[...], ztab_lo[...])
            line = jnp.sum(box * col_mask[...], axis=0, keepdims=True)
            result = result + jnp.where(sub8 == 2 * h + p, line, 0.0)
            result = result + jnp.where(sub8 == 2 * h + p + 4, -turn(line), 0.0)
        return result

    def forward(vector, n, h):
        send[n, h] = spread([vector[2 * h + p : 2 * h + p + 1] for p in range(2)])
        exchange(send.at[n, h], recv.at[n, h], 17 + 2 * n + h)

    def arrived(n, h):
        exchanged(recv.at[n, h], 17 + 2 * n + h)
        return recv[n, h]

    def backward(values, factor, n, h):
        send[n, h] = from_planes(values, factor)
        exchange(send.at[n, h], recv.at[n, h], 17 + 2 * n + h)

    def correlate(vector, n):
        high = vector.astype(BF16).astype(F32)
        both = jnp.concatenate([high, vector - high], axis=0).astype(BF16)
        first = dot(both, gath_hi[...], 1, 1)
        second = dot(both, gath_lo[...], 1, 1)
        total = first[:8] + first[8:] + second[:8]
        for k in range(4):
            pair_send[n, k] = total[:, 128 * k : 128 * k + 128]

    sign = jnp.where(sub8 < 4, 1.0, -1.0)

    def expand(correlations):
        high = correlations.astype(BF16).astype(F32)
        both = jnp.concatenate([high, correlations - high], axis=0).astype(BF16)
        first = dot(both, gath_hi[...], 1, 0)
        second = dot(both, gath_lo[...], 1, 0)
        direct = first[:8] + first[8:] + second[:8]
        return (direct + sign * turn(pltpu.roll(direct, 4, 0))) * (1.0 / (2.0 * NPW))

    lane = lax.broadcasted_iota(jnp.int32, (1, 128), 1)

    def per_lane(column, h):
        return jnp.where(lane < 64, column[2 * h : 2 * h + 1], column[2 * h + 1 : 2 * h + 2])

    def as_row(columns):
        total = jnp.zeros((8, 128), F32)
        for k, column in enumerate(columns):
            total = total + jnp.where(lane == sub8 + 8 * k, column, 0.0)
        return jnp.sum(total, axis=0, keepdims=True)

    def as_column(row, k):
        return jnp.sum(jnp.where(lane == sub8 + 8 * k, row, 0.0), axis=1, keepdims=True)

    def over_lanes(value):
        return jnp.sum(value, axis=1, keepdims=True)

    def to_all_bands(src, dst, slot, rows):
        def go(k, carry):
            peer = band_peer(k)
            part = src if rows is None else src.at[pl.ds(pl.multiple_of(rows * peer, rows), rows)]
            place = dst.at[r] if rows is None else dst.at[pl.ds(pl.multiple_of(rows * r, rows), rows)]
            pltpu.make_async_remote_copy(
                src_ref=part, dst_ref=place, send_sem=ssem.at[slot], recv_sem=rsem.at[slot],
                device_id={"band": peer}, device_id_type=MESH,
            ).start()
            return carry

        lax.fori_loop(0, BANDS - 1, go, 0)

    def give_density(n, slot):
        to_all_bands(den_send.at[n], den_recv.at[n], slot, 8)
        sent.append((den_send.at[n, pl.ds(0, 8 * (BANDS - 1))], ssem.at[slot]))
        here = pl.ds(pl.multiple_of(8 * r, 8), 8)
        den_recv[n, here, :] = den_send[n, here, :]

    def overlap(n, h, real, imag):
        den_send[n, :, 128 * h : 128 * h + 128] = 2.0 * (own_field[:256] * real + own_field[256:] * imag)

    gather_0()
    taken(own, rsem.at[0])
    own_row = jnp.concatenate([own[0:1, :], own[1:2, :]], axis=1)
    own_send[...] = spread([own_row, own_row])
    exchange(own_send, own_recv, 1)
    gather_second(1)
    gather_1()
    gather_second(2)
    gather_first(1, 0)
    gather_first(1, 1)
    exchanged(own_recv, 1)
    own_field[...] = to_planes(own_recv[...], o_hi, o_lo)

    for h in range(2):
        backward(own_field[...], trial[:, 128 * h : 128 * h + 128], 0, h)
    gather_second(3)
    gather_first(2, 0)
    gather_second(4)
    gather_first(2, 1)
    gather_first(3, 0)
    gather_first(3, 1)
    source = pick(arrived(0, 0), jnp.zeros((8, 2 * NJ), F32), 0)
    source = pick(arrived(0, 1), source, 1)
    gather_last()

    def round_pair(k, carry):
        rows = pl.ds(pl.multiple_of(16 * k, 16), 16)
        from_rows = pl.ds(pl.multiple_of(16 * (k % ZS), 16), 16)
        gath_hi[rows, :CUT], gath_lo[rows, :CUT] = split(gath_x[k // ZS, from_rows, :])
        gath_hi[rows, CUT:], gath_lo[rows, CUT:] = split(gath_z[k // ZS, from_rows, :])
        return carry

    lax.fori_loop(0, 32, round_pair, 0)
    correlate(source, 0)
    across_chip(0, 3)
    across_ring(0, 4, 3)
    share(0, half_sum(0, 4), 6)
    direction = expand(shared(0, 6)) - source

    for h in range(2):
        forward(direction, 1, h)
    correlate(direction, 1)
    across_chip(1, 8)
    across_ring(1, 11, 8)
    local = pot[...]
    for h in range(2):
        field[0, h] = to_planes(arrived(1, h), y_hi, y_lo)
        backward(field[0, h], local, 2, h)
    corr_dir = half_sum(1, 11)
    share(1, corr_dir, 14)
    for h in range(2):
        overlap(0, h, field[0, h, :256], field[0, h, 256:])
    give_density(0, 13)
    image = diag * direction + 2.0 * expand(shared(1, 14))

    for h in range(2):
        image = pick(arrived(2, h), image, h)
        forward(image, 3, h)
    dots = [over_lanes(direction * direction), over_lanes(direction * image), over_lanes(image * image)]
    sums(0, as_row(dots), 10)
    correlate(image, 2)
    across_chip(2, 15)
    across_ring(2, 16, 15)
    for h in range(2):
        field[1, h] = to_planes(arrived(3, h), y_hi, y_lo)
        overlap(1, h, field[1, h, :256], field[1, h, 256:])
    give_density(1, 9)
    dots = summed(0, 10)
    norm, curve, square = (as_column(dots, k) for k in range(3))
    step0 = norm / curve
    norm_next = step0 * step0 * square - norm
    grow = 1.0 + norm_next / norm
    direction1 = grow * direction - step0 * image
    corr_dir1 = grow * corr_dir - step0 * half_sum(2, 16)

    terms = over_lanes(diag * direction1 * direction1)
    corr_terms = over_lanes(jnp.sum(corr_dir1 * corr_dir1, axis=0))
    corr_terms = corr_terms + pltpu.roll(jnp.broadcast_to(corr_terms, (8, 128)), 4, 0)[:, 0:1]
    terms = terms + corr_terms * (2.0 / (2.0 * NPW) / 8.0)
    for h in range(2):
        mixed = per_lane(grow, h) * field[0, h] - per_lane(step0, h) * field[1, h]
        real, imag = mixed[:256], mixed[256:]
        squares = jnp.sum(local * (real * real + imag * imag), axis=0, keepdims=True)
        for p in range(2):
            piece = over_lanes(squares[:, 64 * p : 64 * p + 64])
            terms = terms + jnp.where((sub8 % 4) == 2 * h + p, piece, 0.0)
    sums(1, as_row([terms]), 12)
    step1 = norm_next / as_column(summed(1, 12), 0)
    weights = (step0 + step1 * grow, -(step1 * step0))
    for n in range(2):
        for h in range(2):
            coef_send[2 * n + h : 2 * n + h + 1, :] = per_lane(weights[n], h)
    to_all_bands(coef_send, coef_recv, 5, None)
    sent.append((coef_recv.at[pl.ds(0, BANDS - 1)], ssem.at[5]))
    coef_recv[r] = coef_send[...]
    response = step0 * direction + step1 * direction1
    for ri in range(2):
        dpsi[0, :, ri, :] = response[:PERTS, NJ * ri : NJ * ri + NJ]

    for n, slot in ((0, 13), (1, 9)):
        taken(den_recv.at[n, pl.ds(0, 8 * (BANDS - 1))], rsem.at[slot])
    taken(coef_recv.at[pl.ds(0, BANDS - 1)], rsem.at[5])
    for h in range(2):
        total = jnp.zeros((8, 128), F32)
        for k in range(BANDS):
            for n in range(2):
                piece = den_recv[n, 8 * k : 8 * k + 8, 128 * h : 128 * h + 128]
                total = total + coef_recv[k, 2 * n + h : 2 * n + h + 1, :] * piece
        for p in range(2):
            for half in range(2):
                piece = total[4 * half : 4 * half + 4, 64 * p : 64 * p + 64]
                dens[2 * h + p, :, 64 * half : 64 * half + 64] = piece

    drain()
    drain_own()


def on_device(sphere_index, occupied, energies, local_pot, trial_pot):
    tables = [jnp.asarray(table) for table in make_tables()]
    vmem = pl.BlockSpec(memory_space=pltpu.VMEM)
    far = pl.BlockSpec(memory_space=pl.ANY)
    scratch = [pltpu.VMEM(table.shape, F32) for table in tables[2:]]
    scratch += [pltpu.VMEM(table.shape, BF16) for table in tables[2:] for _ in range(2)]
    scratch += [
        pltpu.VMEM((XS, 128, CUT), F32),
        pltpu.VMEM((XS, 128, 2 * NJ - CUT), F32),
        pltpu.VMEM((512, 2 * NJ), BF16),
        pltpu.VMEM((512, 2 * NJ), BF16),
        pltpu.VMEM((2, NJ), F32),
        pltpu.VMEM((128, 2 * NJ), BF16),
        pltpu.VMEM((128, 2 * NJ), BF16),
        pltpu.VMEM((64, 2 * NJ), F32),
        pltpu.VMEM((128, 2 * NJ), BF16),
        pltpu.VMEM((128, 2 * NJ), BF16),
        pltpu.VMEM((128, 128), F32),
        pltpu.VMEM((128, 128), F32),
        pltpu.VMEM((4, 2, 128, 128), F32),
        pltpu.VMEM((4, 2, 128, 128), F32),
        pltpu.VMEM((3, 4, 8, 128), F32),
        pltpu.VMEM((3, 2, 8, 128), F32),
        pltpu.VMEM((3, 2, 8, 128), F32),
        pltpu.VMEM((3, 8, 2, 8, 128), F32),
        pltpu.VMEM((2, 4, 8, 128), F32),
        pltpu.VMEM((2, 1, 128), F32),
        pltpu.VMEM((2, GRID, 1, 128), F32),
        pltpu.VMEM((2, 256, 256), F32),
        pltpu.VMEM((2, 256, 256), F32),
        pltpu.VMEM((4, 128), F32),
        pltpu.VMEM((BANDS, 4, 128), F32),
        pltpu.VMEM((512, 128), F32),
        pltpu.VMEM((2, 2, 512, 128), F32),
        pltpu.VMEM((256, 128), F32),
        pltpu.VMEM((256, 256), F32),
        pltpu.VMEM(occupied.shape, F32),
        pltpu.VMEM(local_pot.shape, F32),
        pltpu.VMEM(trial_pot.shape, F32),
        pltpu.SemaphoreType.DMA((25,)),
        pltpu.SemaphoreType.DMA((25,)),
        pltpu.SemaphoreType.DMA((4,)),
        pltpu.SemaphoreType.DMA((23,)),
        pltpu.SemaphoreType.DMA((8,)),
    ]
    return pl.pallas_call(
        kernel,
        out_shape=(
            jax.ShapeDtypeStruct((1, PERTS, 2, NJ), F32),
            jax.ShapeDtypeStruct((PERTS, 4, 128), F32),
        ),
        in_specs=[vmem, far, vmem, far, far, vmem, vmem] + [far] * 5,
        out_specs=(vmem, vmem),
        scratch_shapes=scratch,
        compiler_params=pltpu.CompilerParams(
            collective_id=0, has_side_effects=True, vmem_limit_bytes=60 * 1024 * 1024
        ),
        name="response",
    )(sphere_index, occupied, energies, local_pot, trial_pot, *tables)


def solution(mesh):
    return jax.shard_map(
        on_device,
        mesh=mesh,
        in_specs=(
            P("grid"),
            P("band", None, "grid"),
            P("band"),
            P("grid", None),
            P(None, "grid", None),
        ),
        out_specs=(P("band", None, None, "grid"), P(None, "grid", "band")),
        check_vma=False,
    )
```

```python
import numpy as np
import jax
import jax.numpy as jnp
import ml_dtypes
from jax import lax
from jax.experimental import pallas as pl
from jax.experimental.pallas import tpu as pltpu
from jax.sharding import PartitionSpec as P

NG = 64
NPW = 12288
NJ = 768
PERTS = 4
GRID = 16
XS, ZS = 4, 8
CUT = 640
BANDS = 32
KIN_SCALE = 0.02
MESH = pl.DeviceIdType.MESH
F32 = jnp.float32
BF16 = jnp.bfloat16


def halves(table):
    high = table.astype(ml_dtypes.bfloat16)
    low = (table - high.astype(np.float64)).astype(ml_dtypes.bfloat16)
    return high, low


def make_tables():
    freq = np.arange(32) - 32 * (np.arange(32) >= 16)
    norm = 1.0 / np.sqrt(NG)
    angle = 2 * np.pi / NG
    phase = np.exp(1j * angle * np.outer(np.arange(NG), freq)) * norm
    z_tab = np.zeros((NG, 2, 2, 32))
    for ri in range(2):
        value = phase * (1j**ri)
        z_tab[:, 0, ri], z_tab[:, 1, ri] = value.real, value.imag
    z_tab = z_tab.reshape(128, 64)
    y_tab = np.zeros((2, 2, 32, 2, 2, 2, NG))
    own_tab = np.zeros((2, 2, 32, 2, 2, 2, NG))
    for p in range(2):
        for k in range(2):
            y_tab[p, k, :, k, 0, p] = phase.real.T
            y_tab[p, k, :, k, 1, p] = phase.imag.T
            own_tab[0, k, :, k, 0, p] = phase.real.T
            own_tab[0, k, :, k, 1, p] = phase.imag.T
    y_tab = y_tab.reshape(128, 512)
    own_tab = own_tab.reshape(128, 512)
    x_tab = np.zeros((2, 32, 2, 4, 2, 2, GRID, 4, 2))
    for k in range(2):
        rotor = np.exp(1j * angle * np.outer(np.arange(NG), np.arange(GRID) - 16 * k)) * norm
        rotor = rotor.reshape(32, 2, GRID)
        for cs in range(2):
            for ri in range(2):
                value = rotor * (1j ** (cs + ri))
                for zl in range(4):
                    x_tab[0, :, :, zl, k, cs, :, zl, ri] = value.real
                    x_tab[1, :, :, zl, k, cs, :, zl, ri] = value.imag
    x_tab = x_tab.reshape(512, 512)
    return list(halves(z_tab)) + [t.astype(np.float32) for t in (own_tab, x_tab, y_tab, x_tab.T, y_tab.T)]


def split(value):
    high = value.astype(BF16)
    return high, (value - high.astype(F32)).astype(BF16)


def dot(a, b, ca, cb):
    return lax.dot_general(a, b, (((ca,), (cb,)), ((), ())), preferred_element_type=F32)


def dot3(a_high, a_low, b_high, b_low, ca=1, cb=0):
    total = dot(a_high, b_high, ca, cb) + dot(a_low, b_high, ca, cb)
    return total + dot(a_high, b_low, ca, cb)


def turn(vector):
    return jnp.concatenate([-vector[:, NJ:], vector[:, :NJ]], axis=1)


def kernel(
    sph, occ_hbm, energy, pot_hbm, trial_hbm, zt_hi, zt_lo, *refs,
):
    stored, (dpsi, dens), whole, kept, rest = refs[:5], refs[5:7], refs[7:12], refs[12:22], refs[22:]
    o_hi, o_lo, t_hi, t_lo, y_hi, y_lo, tt_hi, tt_lo, yt_hi, yt_lo = kept
    (
    gath_x, gath_z, gath_hi, gath_lo, own, ztab_hi, ztab_lo, col_mask, rhs_hi, rhs_lo,
    own_send, own_recv, send, recv, pair_send, pair_recv, half_send, half_recv, full_recv, sum_send, sum_recv,
    den_send, den_recv, coef_send, coef_recv, own_field, field, pot, trial, occ, pot_in, trial_in, ssem, rsem, gsend, grecv, tsem,
    ) = rest
    g = lax.axis_index("grid")
    r = lax.axis_index("band")
    bx, bz = r // ZS, r % ZS
    gy, gc = g // 2, g % 2

    def ring(j, half):
        return half + (1 - 2 * (j % 2)) * ((j + 1) // 2)

    def grid_peer(k):
        return 2 * ((gy + ring(k // 2, 4)) % 8) + (gc + k + 1) % 2

    def band_peer(k):
        return ZS * ((bx + ring(k % 4, 2)) % XS) + (bz + ring(k // 4, 4)) % ZS

    barrier = pltpu.get_barrier_semaphore()

    def greet_grid(k, carry):
        pl.semaphore_signal(barrier, inc=1, device_id={"grid": grid_peer(k)}, device_id_type=MESH)
        return carry

    def greet_band(k, carry):
        pl.semaphore_signal(barrier, inc=1, device_id={"band": band_peer(k)}, device_id_type=MESH)
        return carry

    lax.fori_loop(0, BANDS - 1, greet_band, 0)
    lax.fori_loop(0, GRID - 1, greet_grid, 0)

    loads = [pltpu.make_async_copy(a, b, tsem.at[k]) for k, (a, b) in enumerate(zip(stored, whole))]
    inputs = ((occ_hbm, occ), (pot_hbm, pot_in), (trial_hbm, trial_in))
    inputs = [pltpu.make_async_copy(a, b, tsem.at[5 + k]) for k, (a, b) in enumerate(inputs)]
    for load in inputs + loads:
        load.start()

    def taken(ref, sem):
        pltpu.make_async_copy(ref, ref, sem).wait()

    sent = []

    def drain():
        for ref, sem in sent:
            taken(ref, sem)

    def to_band(src, dst, send_sem, recv_sem, x, z):
        pltpu.make_async_remote_copy(
            src_ref=src, dst_ref=dst, send_sem=send_sem, recv_sem=recv_sem,
            device_id={"band": x * ZS + z}, device_id_type=MESH,
        ).start()

    place = sph[...].reshape(1, NJ)
    kz, xl, ky = place // 256, (place // 64) % 4, place % 64
    kx = g + 16 * xl

    def wave(k):
        return jnp.where(k < 32, k, k - 64)

    fx, fy, fz = wave(kx), wave(ky), wave(kz)
    kinetic = KIN_SCALE * (fx * fx + fy * fy + fz * fz).astype(F32)
    diag = jnp.concatenate([kinetic, kinetic], axis=1) - energy[...].reshape(1, 1)
    one_z = jnp.where(lax.broadcasted_iota(jnp.int32, (32, NJ), 0) == (kz & 31), 1.0, 0.0).astype(BF16)
    column = (xl >> 1) * 32 + (ky & 31)
    one_col = jnp.where(lax.broadcasted_iota(jnp.int32, (64, NJ), 0) == column, 1.0, 0.0)
    col_mask[:, :NJ] = one_col
    col_mask[:, NJ:] = one_col
    for ri in range(2):
        lanes = pl.ds(ri * NJ, NJ)
        ztab_hi[:, lanes] = dot(zt_hi[:, 32 * ri : 32 * ri + 32], one_z, 1, 0).astype(BF16)
        ztab_lo[:, lanes] = dot(zt_lo[:, 32 * ri : 32 * ri + 32], one_z, 1, 0).astype(BF16)
    for load in inputs:
        load.wait()

    left = lax.broadcasted_iota(jnp.int32, (4, 128), 1) < 64

    def lay(t, carry):
        lanes = pl.ds(pl.multiple_of(128 * t, 128), 128)
        rows = pl.ds(pl.multiple_of(8 * t, 8), 8)
        for q in range(3):
            a, b = (pot_in[:, lanes],) * 2 if q == 2 else (trial_in[2 * q, :, lanes], trial_in[2 * q + 1, :, lanes])
            even = jnp.where(left, a, pltpu.roll(b, 64, 1))
            odd = jnp.where(left, pltpu.roll(a, 64, 1), b)
            both = jnp.concatenate([even, odd], axis=0)
            if q == 2:
                pot[rows, :] = both
            else:
                trial[rows, 128 * q : 128 * q + 128] = both
        return carry

    lax.fori_loop(0, 32, lay, 0)
    mine = jnp.concatenate([occ[:, 0, :], occ[:, 1, :]], axis=1)
    own_z = pl.ds(pl.multiple_of(16 * bz, 16), 16)
    gath_x[bx, own_z, :] = mine[:, :CUT]
    gath_z[bx, own_z, :] = mine[:, CUT:]

    for k, load in enumerate(loads):
        load.wait()
        for i in range(0, whole[k].shape[0], 64):
            high, low = split(whole[k][i : i + 64, :])
            kept[2 * k][i : i + 64, :] = high
            kept[2 * k + 1][i : i + 64, :] = low

    pl.semaphore_wait(barrier, GRID - 1 + BANDS - 1)

    @pl.when(r == 0)
    def _():
        pltpu.make_async_copy(occ.at[0], own, rsem.at[0]).start()

    @pl.when(r < 2)
    def _():
        def give(i, carry):
            pltpu.make_async_remote_copy(
                src_ref=occ.at[i], dst_ref=own, send_sem=ssem.at[0], recv_sem=rsem.at[0],
                device_id={"band": 16 * r + i}, device_id_type=MESH,
            ).start()
            return carry

        lax.fori_loop(jnp.where(r == 0, 1, 0), 16, give, 0)

    def drain_own():
        @pl.when(r == 0)
        def _():
            taken(occ.at[pl.ds(0, 15)], ssem.at[0])

        @pl.when(r == 1)
        def _():
            taken(occ, ssem.at[0])

    def block(part, x, z):
        return (gath_z if part else gath_x).at[x, pl.ds(pl.multiple_of(16 * z, 16), 16)]

    def col(z, first=0, count=XS):
        return gath_x.at[pl.ds(first, count), pl.ds(pl.multiple_of(16 * z, 16), 16)]

    z_up, z_dn = (bz + 1) % ZS, (bz + ZS - 1) % ZS

    def across(part, z, slot):
        for k in (2, 1, 3):
            to_band(block(part, bx, z), block(part, bx, z), gsend.at[slot], grecv.at[slot], (bx + k) % XS, bz)

    def below(d):
        return (bz + ZS - d) % ZS

    def above(d):
        return (bz + d) % ZS

    def first(way, d, half):
        return grecv.at[2 + 7 * way + (6 if d == 4 else 2 * d - 2 + half)]

    def second(way, d):
        return grecv.at[16 + 4 * way + d - 1]

    def send_first(way, z, d, half):
        ref = col(z, 2 * half, 2)
        to_band(ref, ref, gsend.at[2], first(way, d, half), bx, z_dn if way else z_up)

    def send_second(way, z, d):
        to_band(block(1, bx, z), block(1, bx, z), gsend.at[3], second(way, d), bx, z_dn if way else z_up)

    def gather_0():
        across(0, bz, 0)
        for way in range(2):
            send_second(way, bz, 1)
        across(1, bz, 1)
        sent.append((gath_x.at[pl.ds(0, 3), pl.ds(0, 16)], gsend.at[0]))
        sent.append((gath_z.at[pl.ds(0, 3)], gsend.at[1]))
        sent.append((gath_x.at[:, pl.ds(0, 112)], gsend.at[2]))
        sent.append((gath_z.at[0, pl.ds(0, 112)], gsend.at[3]))

    def gather_1():
        taken(gath_x.at[pl.ds(0, 3), pl.ds(0, 16)], grecv.at[0])
        for half in range(2):
            for way in range(2):
                send_first(way, bz, 1, half)

    def gather_first(d, half):
        for way in range(2):
            z = above(d) if way else below(d)
            if d < 3 or half == way:
                taken(col(z, 2 * half, 2), first(way, d, half))
                send_first(way, z, d + 1, half)

    def gather_second(d):
        for way in range(1 if d == 4 else 2):
            z = above(d) if way else below(d)
            taken(block(1, bx, z), second(way, d))
            if d + way < 4:
                send_second(way, z, d + 1)
            across(1, z, 1)

    def gather_last():
        taken(col(below(3), 2, 2), first(0, 3, 1))
        taken(col(above(3), 0, 2), first(1, 3, 0))
        taken(col(below(4), 0, 2), first(0, 4, 0))
        taken(col(below(4), 2, 2), first(1, 4, 1))
        taken(gath_z.at[pl.ds(0, 3)], grecv.at[1])

    def exchange(src, dst, slot):
        def go(k, carry):
            peer = grid_peer(k)
            pltpu.make_async_remote_copy(
                src_ref=src.at[pl.ds(pl.multiple_of(8 * peer, 8), 8)],
                dst_ref=dst.at[pl.ds(pl.multiple_of(8 * g, 8), 8)],
                send_sem=ssem.at[slot], recv_sem=rsem.at[slot],
                device_id={"grid": peer}, device_id_type=MESH,
            ).start()
            return carry

        lax.fori_loop(0, GRID - 1, go, 0)
        sent.append((src.at[pl.ds(0, 8 * (GRID - 1))], ssem.at[slot]))
        here = pl.ds(pl.multiple_of(8 * g, 8), 8)
        dst[here, :] = src[here, :]

    def exchanged(dst, slot):
        taken(dst.at[pl.ds(0, 8 * (GRID - 1))], rsem.at[slot])

    other = 1 - gc

    def to_other(src, dst, slot):
        pltpu.make_async_remote_copy(
            src_ref=src, dst_ref=dst, send_sem=ssem.at[slot], recv_sem=rsem.at[slot],
            device_id={"grid": 2 * gy + other}, device_id_type=MESH,
        ).start()
        sent.append((src, ssem.at[slot]))

    def across_chip(n, slot):
        to_other(pair_send.at[n, pl.ds(2 * other, 2)], pair_recv.at[n], slot)

    def across_ring(n, slot, slot_in):
        taken(pair_recv.at[n], rsem.at[slot_in])
        total = pair_send[n, pl.ds(2 * gc, 2)] + pair_recv[n]
        half_send[n] = total

        def go(k, carry):
            pltpu.make_async_remote_copy(
                src_ref=half_send.at[n], dst_ref=half_recv.at[n, gy],
                send_sem=ssem.at[slot], recv_sem=rsem.at[slot],
                device_id={"grid": 2 * ((gy + ring(k, 4)) % 8) + gc}, device_id_type=MESH,
            ).start()
            return carry

        lax.fori_loop(0, 7, go, 0)
        sent.append((half_recv.at[n, pl.ds(0, 7)], ssem.at[slot]))
        half_recv[n, gy] = total

    def half_sum(n, slot):
        taken(half_recv.at[n, pl.ds(0, 7)], rsem.at[slot])
        return jnp.sum(half_recv[n], axis=0)

    def share(n, total, slot):
        full_recv[n, pl.ds(2 * gc, 2)] = total
        to_other(full_recv.at[n, pl.ds(2 * gc, 2)], full_recv.at[n, pl.ds(2 * gc, 2)], slot)

    def shared(n, slot):
        taken(full_recv.at[n, pl.ds(0, 2)], rsem.at[slot])
        return jnp.concatenate([full_recv[n, k] for k in range(4)], axis=1)

    def sums(n, value, slot):
        sum_send[n] = value

        def go(k, carry):
            pltpu.make_async_remote_copy(
                src_ref=sum_send.at[n], dst_ref=sum_recv.at[n, g],
                send_sem=ssem.at[slot], recv_sem=rsem.at[slot],
                device_id={"grid": grid_peer(k)}, device_id_type=MESH,
            ).start()
            return carry

        lax.fori_loop(0, GRID - 1, go, 0)
        sent.append((sum_recv.at[n, pl.ds(0, GRID - 1)], ssem.at[slot]))
        sum_recv[n, g] = value

    def summed(n, slot):
        taken(sum_recv.at[n, pl.ds(0, GRID - 1)], rsem.at[slot])
        return jnp.sum(sum_recv[n], axis=0)

    def spread(rows):
        mask = col_mask[...]
        for p, row in enumerate(rows):
            high = row.astype(BF16).astype(F32)
            rhs_hi[64 * p : 64 * p + 64, :] = (mask * high).astype(BF16)
            rhs_lo[64 * p : 64 * p + 64, :] = (mask * (row - high)).astype(BF16)
        return dot3(ztab_hi[...], ztab_lo[...], rhs_hi[...], rhs_lo[...], 1, 1)

    def to_planes(spectral, yh, yl):
        high, low = split(spectral)
        part = dot3(high, low, yh[...], yl[...])
        part = jnp.concatenate([part[:, 128 * k : 128 * k + 128] for k in range(4)], axis=0)
        high, low = split(part)
        return dot3(t_hi[...], t_lo[...], high, low)

    def from_planes(values, factor):
        values = jnp.concatenate([values[:256] * factor, values[256:] * factor], axis=0)
        high, low = split(values)
        part = dot3(tt_hi[...], tt_lo[...], high, low)
        part = jnp.concatenate([part[128 * k : 128 * k + 128] for k in range(4)], axis=1)
        high, low = split(part)
        return dot3(high, low, yt_hi[...], yt_lo[...])

    sub8 = lax.broadcasted_iota(jnp.int32, (8, 1), 0)

    def pick(spectral, start, h):
        high, low = split(jnp.transpose(spectral))
        result = start
        for p in range(2):
            rows = slice(64 * p, 64 * p + 64)
            box = dot3(high[rows], low[rows], ztab_hi[...], ztab_lo[...])
            line = jnp.sum(box * col_mask[...], axis=0, keepdims=True)
            result = result + jnp.where(sub8 == 2 * h + p, line, 0.0)
            result = result + jnp.where(sub8 == 2 * h + p + 4, -turn(line), 0.0)
        return result

    def forward(vector, n, h):
        send[n, h] = spread([vector[2 * h + p : 2 * h + p + 1] for p in range(2)])
        exchange(send.at[n, h], recv.at[n, h], 17 + 2 * n + h)

    def arrived(n, h):
        exchanged(recv.at[n, h], 17 + 2 * n + h)
        return recv[n, h]

    def backward(values, factor, n, h):
        send[n, h] = from_planes(values, factor)
        exchange(send.at[n, h], recv.at[n, h], 17 + 2 * n + h)

    def correlate(vector, n):
        high = vector.astype(BF16).astype(F32)
        both = jnp.concatenate([high, vector - high], axis=0).astype(BF16)
        first = dot(both, gath_hi[...], 1, 1)
        second = dot(both, gath_lo[...], 1, 1)
        total = first[:8] + first[8:] + second[:8]
        for k in range(4):
            pair_send[n, k] = total[:, 128 * k : 128 * k + 128]

    sign = jnp.where(sub8 < 4, 1.0, -1.0)

    def expand(correlations):
        high = correlations.astype(BF16).astype(F32)
        both = jnp.concatenate([high, correlations - high], axis=0).astype(BF16)
        first = dot(both, gath_hi[...], 1, 0)
        second = dot(both, gath_lo[...], 1, 0)
        direct = first[:8] + first[8:] + second[:8]
        return (direct + sign * turn(pltpu.roll(direct, 4, 0))) * (1.0 / (2.0 * NPW))

    lane = lax.broadcasted_iota(jnp.int32, (1, 128), 1)

    def per_lane(column, h):
        return jnp.where(lane < 64, column[2 * h : 2 * h + 1], column[2 * h + 1 : 2 * h + 2])

    def as_row(columns):
        total = jnp.zeros((8, 128), F32)
        for k, column in enumerate(columns):
            total = total + jnp.where(lane == sub8 + 8 * k, column, 0.0)
        return jnp.sum(total, axis=0, keepdims=True)

    def as_column(row, k):
        return jnp.sum(jnp.where(lane == sub8 + 8 * k, row, 0.0), axis=1, keepdims=True)

    def over_lanes(value):
        return jnp.sum(value, axis=1, keepdims=True)

    def to_all_bands(src, dst, slot, rows):
        def go(k, carry):
            peer = band_peer(k)
            part = src if rows is None else src.at[pl.ds(pl.multiple_of(rows * peer, rows), rows)]
            place = dst.at[r] if rows is None else dst.at[pl.ds(pl.multiple_of(rows * r, rows), rows)]
            pltpu.make_async_remote_copy(
                src_ref=part, dst_ref=place, send_sem=ssem.at[slot], recv_sem=rsem.at[slot],
                device_id={"band": peer}, device_id_type=MESH,
            ).start()
            return carry

        lax.fori_loop(0, BANDS - 1, go, 0)

    def give_density(n, slot):
        to_all_bands(den_send.at[n], den_recv.at[n], slot, 8)
        sent.append((den_send.at[n, pl.ds(0, 8 * (BANDS - 1))], ssem.at[slot]))
        here = pl.ds(pl.multiple_of(8 * r, 8), 8)
        den_recv[n, here, :] = den_send[n, here, :]

    def overlap(n, h, real, imag):
        den_send[n, :, 128 * h : 128 * h + 128] = 2.0 * (own_field[:256] * real + own_field[256:] * imag)

    gather_0()
    taken(own, rsem.at[0])
    own_row = jnp.concatenate([own[0:1, :], own[1:2, :]], axis=1)
    own_send[...] = spread([own_row, own_row])
    exchange(own_send, own_recv, 1)
    gather_1()
    gather_second(1)
    gather_first(1, 0)
    gather_second(2)
    gather_first(1, 1)
    exchanged(own_recv, 1)
    own_field[...] = to_planes(own_recv[...], o_hi, o_lo)

    for h in range(2):
        backward(own_field[...], trial[:, 128 * h : 128 * h + 128], 0, h)
    gather_first(2, 0)
    gather_second(3)
    gather_first(2, 1)
    gather_second(4)
    gather_first(3, 0)
    gather_first(3, 1)
    source = pick(arrived(0, 0), jnp.zeros((8, 2 * NJ), F32), 0)
    source = pick(arrived(0, 1), source, 1)
    gather_last()

    def round_pair(k, carry):
        rows = pl.ds(pl.multiple_of(16 * k, 16), 16)
        from_rows = pl.ds(pl.multiple_of(16 * (k % ZS), 16), 16)
        gath_hi[rows, :CUT], gath_lo[rows, :CUT] = split(gath_x[k // ZS, from_rows, :])
        gath_hi[rows, CUT:], gath_lo[rows, CUT:] = split(gath_z[k // ZS, from_rows, :])
        return carry

    lax.fori_loop(0, 32, round_pair, 0)
    correlate(source, 0)
    across_chip(0, 3)
    across_ring(0, 4, 3)
    share(0, half_sum(0, 4), 6)
    direction = expand(shared(0, 6)) - source

    for h in range(2):
        forward(direction, 1, h)
    correlate(direction, 1)
    across_chip(1, 8)
    across_ring(1, 11, 8)
    local = pot[...]
    for h in range(2):
        field[0, h] = to_planes(arrived(1, h), y_hi, y_lo)
        backward(field[0, h], local, 2, h)
    corr_dir = half_sum(1, 11)
    share(1, corr_dir, 14)
    for h in range(2):
        overlap(0, h, field[0, h, :256], field[0, h, 256:])
    give_density(0, 13)
    image = diag * direction + 2.0 * expand(shared(1, 14))

    for h in range(2):
        image = pick(arrived(2, h), image, h)
        forward(image, 3, h)
    dots = [over_lanes(direction * direction), over_lanes(direction * image), over_lanes(image * image)]
    sums(0, as_row(dots), 10)
    correlate(image, 2)
    across_chip(2, 15)
    across_ring(2, 16, 15)
    for h in range(2):
        field[1, h] = to_planes(arrived(3, h), y_hi, y_lo)
        overlap(1, h, field[1, h, :256], field[1, h, 256:])
    give_density(1, 9)
    dots = summed(0, 10)
    norm, curve, square = (as_column(dots, k) for k in range(3))
    step0 = norm / curve
    norm_next = step0 * step0 * square - norm
    grow = 1.0 + norm_next / norm
    direction1 = grow * direction - step0 * image
    corr_dir1 = grow * corr_dir - step0 * half_sum(2, 16)

    terms = over_lanes(diag * direction1 * direction1)
    corr_terms = over_lanes(jnp.sum(corr_dir1 * corr_dir1, axis=0))
    corr_terms = corr_terms + pltpu.roll(jnp.broadcast_to(corr_terms, (8, 128)), 4, 0)[:, 0:1]
    terms = terms + corr_terms * (2.0 / (2.0 * NPW) / 8.0)
    for h in range(2):
        mixed = per_lane(grow, h) * field[0, h] - per_lane(step0, h) * field[1, h]
        real, imag = mixed[:256], mixed[256:]
        squares = jnp.sum(local * (real * real + imag * imag), axis=0, keepdims=True)
        for p in range(2):
            piece = over_lanes(squares[:, 64 * p : 64 * p + 64])
            terms = terms + jnp.where((sub8 % 4) == 2 * h + p, piece, 0.0)
    sums(1, as_row([terms]), 12)
    step1 = norm_next / as_column(summed(1, 12), 0)
    weights = (step0 + step1 * grow, -(step1 * step0))
    for n in range(2):
        for h in range(2):
            coef_send[2 * n + h : 2 * n + h + 1, :] = per_lane(weights[n], h)
    to_all_bands(coef_send, coef_recv, 5, None)
    coef_recv[r] = coef_send[...]
    response = step0 * direction + step1 * direction1
    for ri in range(2):
        dpsi[0, :, ri, :] = response[:PERTS, NJ * ri : NJ * ri + NJ]

    drain()
    drain_own()

    for n, slot in ((0, 13), (1, 9)):
        taken(den_recv.at[n, pl.ds(0, 8 * (BANDS - 1))], rsem.at[slot])
    taken(coef_recv.at[pl.ds(0, BANDS - 1)], rsem.at[5])
    for h in range(2):
        total = jnp.zeros((8, 128), F32)
        for k in range(BANDS):
            for n in range(2):
                piece = den_recv[n, 8 * k : 8 * k + 8, 128 * h : 128 * h + 128]
                total = total + coef_recv[k, 2 * n + h : 2 * n + h + 1, :] * piece
        for p in range(2):
            for half in range(2):
                piece = total[4 * half : 4 * half + 4, 64 * p : 64 * p + 64]
                dens[2 * h + p, :, 64 * half : 64 * half + 64] = piece

    taken(coef_recv.at[pl.ds(0, BANDS - 1)], ssem.at[5])


def on_device(sphere_index, occupied, energies, local_pot, trial_pot):
    tables = [jnp.asarray(table) for table in make_tables()]
    vmem = pl.BlockSpec(memory_space=pltpu.VMEM)
    far = pl.BlockSpec(memory_space=pl.ANY)
    scratch = [pltpu.VMEM(table.shape, F32) for table in tables[2:]]
    scratch += [pltpu.VMEM(table.shape, BF16) for table in tables[2:] for _ in range(2)]
    scratch += [
        pltpu.VMEM((XS, 128, CUT), F32),
        pltpu.VMEM((XS, 128, 2 * NJ - CUT), F32),
        pltpu.VMEM((512, 2 * NJ), BF16),
        pltpu.VMEM((512, 2 * NJ), BF16),
        pltpu.VMEM((2, NJ), F32),
        pltpu.VMEM((128, 2 * NJ), BF16),
        pltpu.VMEM((128, 2 * NJ), BF16),
        pltpu.VMEM((64, 2 * NJ), F32),
        pltpu.VMEM((128, 2 * NJ), BF16),
        pltpu.VMEM((128, 2 * NJ), BF16),
        pltpu.VMEM((128, 128), F32),
        pltpu.VMEM((128, 128), F32),
        pltpu.VMEM((4, 2, 128, 128), F32),
        pltpu.VMEM((4, 2, 128, 128), F32),
        pltpu.VMEM((3, 4, 8, 128), F32),
        pltpu.VMEM((3, 2, 8, 128), F32),
        pltpu.VMEM((3, 2, 8, 128), F32),
        pltpu.VMEM((3, 8, 2, 8, 128), F32),
        pltpu.VMEM((2, 4, 8, 128), F32),
        pltpu.VMEM((2, 1, 128), F32),
        pltpu.VMEM((2, GRID, 1, 128), F32),
        pltpu.VMEM((2, 256, 256), F32),
        pltpu.VMEM((2, 256, 256), F32),
        pltpu.VMEM((4, 128), F32),
        pltpu.VMEM((BANDS, 4, 128), F32),
        pltpu.VMEM((512, 128), F32),
        pltpu.VMEM((2, 2, 512, 128), F32),
        pltpu.VMEM((256, 128), F32),
        pltpu.VMEM((256, 256), F32),
        pltpu.VMEM(occupied.shape, F32),
        pltpu.VMEM(local_pot.shape, F32),
        pltpu.VMEM(trial_pot.shape, F32),
        pltpu.SemaphoreType.DMA((25,)),
        pltpu.SemaphoreType.DMA((25,)),
        pltpu.SemaphoreType.DMA((4,)),
        pltpu.SemaphoreType.DMA((23,)),
        pltpu.SemaphoreType.DMA((8,)),
    ]
    return pl.pallas_call(
        kernel,
        out_shape=(
            jax.ShapeDtypeStruct((1, PERTS, 2, NJ), F32),
            jax.ShapeDtypeStruct((PERTS, 4, 128), F32),
        ),
        in_specs=[vmem, far, vmem, far, far, vmem, vmem] + [far] * 5,
        out_specs=(vmem, vmem),
        scratch_shapes=scratch,
        compiler_params=pltpu.CompilerParams(
            collective_id=0, has_side_effects=True, vmem_limit_bytes=60 * 1024 * 1024
        ),
        name="response",
    )(sphere_index, occupied, energies, local_pot, trial_pot, *tables)


def solution(mesh):
    return jax.shard_map(
        on_device,
        mesh=mesh,
        in_specs=(
            P("grid"),
            P("band", None, "grid"),
            P("band"),
            P("grid", None),
            P(None, "grid", None),
        ),
        out_specs=(P("band", None, None, "grid"), P(None, "grid", "band")),
        check_vma=False,
    )
```
